128 devices in a mesh: section: 2 (over core), row: 4 (over x), col: 16 (over z, y).
Axes of the slice: x: 4, y: 4, z: 4, core: 2. Of those that a mesh axis runs over, the one named last changes fastest.
Arguments:
- pair_act: bfloat16 [2, 2, 256, 256, 128], P('section', None, 'row', 'col'), may hold values from -6 to 6
- pair_cot: float32 [2, 256, 256, 128], P(None, 'row', 'col'), may hold values from -6 to 6
- pad_mask: int32 [2, 256], replicated, may hold values 0 or 1
- ln_gain: float32 [2, 128], P('section'), may hold values from 0.25 to 1.75
- ln_bias: float32 [2, 128], P('section'), may hold values from -3 to 3
- proj_weight: bfloat16 [2, 128, 512], P('section'), may hold values from -0.5 to 0.5
- gate_weight: bfloat16 [2, 128, 128], P('section'), may hold values from -0.5 to 0.5
- out_gain: float32 [2, 128], P('section'), may hold values from 0.25 to 1.75
- out_bias: float32 [2, 128], P('section'), may hold values from -3 to 3
- out_weight: bfloat16 [2, 128, 128], P('section'), may hold values from -0.5 to 0.5
Outputs:
- pair_grad: float32 [2, 2, 256, 256, 128], P('section', None, 'row', 'col')
- grad_ln_gain: float32 [2, 128], P('section')
- grad_ln_bias: float32 [2, 128], P('section')
- grad_proj: float32 [2, 128, 512], P('section')
- grad_gate: float32 [2, 128, 128], P('section')
- grad_out_gain: float32 [2, 128], P('section')
- grad_out_bias: float32 [2, 128], P('section')
- grad_out_weight: float32 [2, 128, 128], P('section')
The draws below stay inside these ranges and needn't reach their ends.
Inputs may be any that keep to these rules, and one draw needn't show every extreme that they name: `pad_mask`: 1 marks a real token, 0 a padding one.
All inputs are finite; a program needn't handle non-finite values.
Results may differ from the reference program's by a relative error of at most 0.0068.
Values may be sent and summed in bfloat16 or wider, within the bound.
A program may use at most 128 MiB of HBM per device.

```python
import functools
import jax
import jax.numpy as jnp
from jax import lax

C = 128
H = 128
TOKENS = 256
MICRO = 2
SECTIONS = 2


def plant(values, own_key, smallest, largest):
    dims = values.shape
    index_at = [jax.random.randint(jax.random.fold_in(own_key, axis), (), 0, dims[axis]) for axis in range(len(dims))]
    values = values.at[tuple(index_at)].set(smallest)
    longest = dims.index(max(dims))
    index_at[longest] = (index_at[longest] + 1) % dims[longest]
    return values.at[tuple(index_at)].set(largest)


def steps_of(own_key, extent, shards, least, top_value):
    def one(dim, blocks):
        draws = jax.random.uniform(jax.random.fold_in(jax.random.fold_in(own_key, 6), dim), (blocks,), jnp.float32, least / len(shards), top_value / len(shards))
        return jnp.repeat(jnp.exp(draws), extent[dim] // blocks).reshape((-1,) + (1,) * (len(extent) - dim - 1))

    gain = one(*shards[0])
    for cut in shards[1:]:
        gain = gain * one(*cut)
    return gain


def normal_values(key, shape, scale, reach, split=(), held_as=jnp.bfloat16):
    values = jax.random.normal(key, shape, jnp.float32) * scale
    if len(split) > 0:
        values = steps_of(key, shape, split, -0.22, 0.18) * values
    return jnp.clip(values, min=-reach, max=reach).astype(held_as)


def setup_inputs(seed: int = 0) -> dict:
    keys = jax.random.split(jax.random.key(seed), 11)
    pair_act = normal_values(keys[0], (SECTIONS, MICRO, TOKENS, TOKENS, C), 1.0, 6.0, ((0, 2), (2, 4), (3, 16)))
    pair_cot = normal_values(keys[1], (MICRO, TOKENS, TOKENS, C), 1.0, 6.0, ((1, 4), (2, 16)), jnp.float32)
    pad_mask = plant((jax.random.randint(keys[2], (MICRO, TOKENS), 0, 8) < 7).astype(jnp.int32), jax.random.fold_in(keys[2], 1), 0, 1)
    ln_gain = jnp.clip(1.0 + 0.15 * jax.random.normal(keys[3], (SECTIONS, C), jnp.float32), 0.25, 1.75)
    ln_bias = normal_values(keys[4], (SECTIONS, C), 0.5, 3.0, ((0, 2),), jnp.float32)
    proj_weight = normal_values(keys[5], (SECTIONS, C, 4 * H), C ** -0.5, 0.5, ((0, 2),))
    gate_weight = normal_values(keys[6], (SECTIONS, C, C), C ** -0.5, 0.5, ((0, 2),))
    out_gain = jnp.clip(1.0 + 0.15 * jax.random.normal(keys[7], (SECTIONS, H), jnp.float32), 0.25, 1.75)
    out_bias = normal_values(keys[8], (SECTIONS, H), 0.5, 3.0, ((0, 2),), jnp.float32)
    out_weight = normal_values(keys[9], (SECTIONS, H, C), H ** -0.5, 0.5, ((0, 2),))
    return dict(pair_act=pair_act, pair_cot=pair_cot, pad_mask=pad_mask, ln_gain=ln_gain, ln_bias=ln_bias, proj_weight=proj_weight, gate_weight=gate_weight, out_gain=out_gain, out_bias=out_bias, out_weight=out_weight)


EPSILON = 1e-05

def layer_norm(values):
    average = lax.optimization_barrier(jnp.mean(values, axis=-1, keepdims=True))
    centred = values - average
    variance = lax.optimization_barrier(jnp.mean(centred * centred, axis=-1, keepdims=True))
    inverse = lax.rsqrt(variance + EPSILON)
    return (centred * inverse, inverse)

def norm_back(grad_hat, normed, inverse):
    first = lax.optimization_barrier(jnp.mean(grad_hat, axis=-1, keepdims=True))
    second = lax.optimization_barrier(jnp.mean(grad_hat * normed, axis=-1, keepdims=True))
    return (grad_hat - first - normed * second) * inverse

def front_part(pair_in, cell_mask, gain_in, bias_in, weight_proj, weight_gate):
    pair_hat, pair_inv = layer_norm(pair_in.astype(jnp.float32))
    normed = (pair_hat * gain_in + bias_in).astype(jnp.bfloat16)
    flat_in = normed.reshape(-1, normed.shape[-1])
    shape_lead = normed.shape[:-1]
    hidden = weight_proj.shape[1] // 4
    projected = jnp.dot(flat_in, weight_proj, preferred_element_type=jnp.float32).reshape(shape_lead + (4 * hidden,))
    lin_a = projected[..., :hidden]
    gate_a = jax.nn.sigmoid(projected[..., hidden:2 * hidden])
    lin_b = projected[..., 2 * hidden:3 * hidden]
    gate_b = jax.nn.sigmoid(projected[..., 3 * hidden:])
    masked = cell_mask[..., None]
    left_proj = (gate_a * lin_a * masked).astype(jnp.bfloat16)
    right_proj = (gate_b * lin_b * masked).astype(jnp.bfloat16)
    gate_out = jax.nn.sigmoid(jnp.dot(flat_in, weight_gate, preferred_element_type=jnp.float32).reshape(shape_lead + (weight_gate.shape[1],)))
    saved = (pair_hat, pair_inv, flat_in, lin_a, gate_a, lin_b, gate_b)
    return (left_proj, right_proj, gate_out, saved)

def out_part(pair_mix, upstream, gate_out, gain_out, bias_out, weight_out):
    mix_hat, mix_inv = layer_norm(pair_mix)
    mixed = (mix_hat * gain_out + bias_out).astype(jnp.bfloat16)
    flat_mix = mixed.reshape(-1, mixed.shape[-1])
    pair_width = weight_out.shape[1]
    outcome = jnp.dot(flat_mix, weight_out, preferred_element_type=jnp.float32).reshape(upstream.shape)
    d_outcome = (upstream * gate_out).astype(jnp.bfloat16)
    d_gate = upstream * outcome * gate_out * (1.0 - gate_out)
    flat_dout = d_outcome.reshape(-1, pair_width)
    d_mixed = lax.dot_general(flat_dout, weight_out, (((1,), (1,)), ((), ())), preferred_element_type=jnp.float32).reshape(mix_hat.shape)
    g_weight = lax.dot_general(flat_mix, flat_dout, (((0,), (0,)), ((), ())), preferred_element_type=jnp.float32)
    hidden = mix_hat.shape[-1]
    g_gain = lax.optimization_barrier(jnp.sum((d_mixed * mix_hat).reshape(-1, hidden), axis=0))
    g_bias = lax.optimization_barrier(jnp.sum(d_mixed.reshape(-1, hidden), axis=0))
    d_mix = norm_back(d_mixed * gain_out, mix_hat, mix_inv).astype(jnp.bfloat16)
    return (d_mix, d_gate, (g_gain, g_bias, g_weight))

def in_part(d_left, d_right, d_gate, saved, cell_mask, upstream, gain_in, joined):
    pair_hat, pair_inv, flat_in, lin_a, gate_a, lin_b, gate_b = saved
    masked = cell_mask[..., None]
    pieces = [d_left * gate_a * masked, d_left * lin_a * masked * gate_a * (1.0 - gate_a), d_right * gate_b * masked, d_right * lin_b * masked * gate_b * (1.0 - gate_b), d_gate]
    d_pre = jnp.concatenate(pieces, axis=-1).astype(jnp.bfloat16)
    flat_dpre = d_pre.reshape(-1, d_pre.shape[-1])
    d_normed = lax.dot_general(flat_dpre, joined, (((1,), (1,)), ((), ())), preferred_element_type=jnp.float32).reshape(pair_hat.shape)
    g_joined = lax.dot_general(flat_in, flat_dpre, (((0,), (0,)), ((), ())), preferred_element_type=jnp.float32)
    pair_width = pair_hat.shape[-1]
    split_at = joined.shape[1] - pair_width
    g_gain = lax.optimization_barrier(jnp.sum((d_normed * pair_hat).reshape(-1, pair_width), axis=0))
    g_bias = lax.optimization_barrier(jnp.sum(d_normed.reshape(-1, pair_width), axis=0))
    d_pair = norm_back(d_normed * gain_in, pair_hat, pair_inv)
    return (upstream + d_pair, (g_gain, g_bias, g_joined[:, :split_at], g_joined[:, split_at:]))

def segment_grad(pair_in, upstream, mask_vec, weights):
    gain_in, bias_in, weight_proj, weight_gate, gain_out, bias_out, weight_out = weights
    cell_mask = mask_vec[:, None] * mask_vec[None, :]
    left_proj, right_proj, gate_out, saved = front_part(pair_in, cell_mask, gain_in, bias_in, weight_proj, weight_gate)
    left_full = left_proj.astype(jnp.float32)
    right_full = right_proj.astype(jnp.float32)
    pair_mix = jnp.einsum('ikh,jkh->ijh', left_full, right_full)
    d_mix, d_gate, out_grads = out_part(pair_mix, upstream, gate_out, gain_out, bias_out, weight_out)
    d_full = d_mix.astype(jnp.float32)
    d_left = jnp.einsum('ijh,jkh->ikh', d_full, right_full)
    d_right = jnp.einsum('ijh,ikh->jkh', d_full, left_full)
    joined = jnp.concatenate([weight_proj, weight_gate], axis=1)
    new_grad, in_grads = in_part(d_left, d_right, d_gate, saved, cell_mask, upstream, gain_in, joined)
    return (new_grad, in_grads + out_grads)

def reference(pair_act, pair_cot, pad_mask, ln_gain, ln_bias, proj_weight, gate_weight, out_gain, out_bias, out_weight):
    segment_total = pair_act.shape[0]
    micro_count = pair_act.shape[1]
    upstream_list = [pair_cot[micro_num] for micro_num in range(micro_count)]
    results = [None] * segment_total
    totals = [None] * segment_total
    for segment_num in range(segment_total - 1, -1, -1):
        weights = (ln_gain[segment_num], ln_bias[segment_num], proj_weight[segment_num], gate_weight[segment_num], out_gain[segment_num], out_bias[segment_num], out_weight[segment_num])
        new_list = []
        grad_list = []
        for micro_num in range(micro_count):
            new_grad, grads = segment_grad(pair_act[segment_num, micro_num], upstream_list[micro_num], pad_mask[micro_num].astype(jnp.float32), weights)
            new_list.append(new_grad)
            grad_list.append(grads)
        results[segment_num] = jnp.stack(new_list)
        totals[segment_num] = tuple((functools.reduce(jnp.add, [entry[number] for entry in grad_list]) for number in range(7)))
        upstream_list = new_list
    stacked = [jnp.stack([entry[number] for entry in totals]) for number in range(7)]
    pair_grad = jnp.stack(results)
    return (pair_grad, stacked[0], stacked[1], stacked[2], stacked[3], stacked[4], stacked[5], stacked[6])
```

```python
import jax
import jax.numpy as jnp
from jax import lax
from jax.experimental import pallas as pl
from jax.experimental.pallas import tpu as pltpu
from jax.sharding import PartitionSpec as P

EPSILON = 1e-05
MESH = pl.DeviceIdType.MESH
F32 = jnp.float32
BF16 = jnp.bfloat16
ROWS = 4
COLS = 16
PEERS = ROWS * COLS
N = 1024
WIDE = 256

X_COPY, W_COPY, O_COPY, V_COPY, PG_COPY = range(5)
LR, MIX, DMIX, DLR, RS = range(5)


def sigmoid(v):
    return 0.5 * jnp.tanh(0.5 * v) + 0.5


def mean0(v):
    return jnp.mean(v, axis=0, keepdims=True)


def dot(a, b, ca=1, cb=0):
    return lax.dot_general(a, b, (((ca,), (cb,)), ((), ())), preferred_element_type=F32)


def kernel(
    act_ref, cot_ref, mask_v, mask_sm, lng_ref, lnb_ref, proj_ref, gatew_ref, og_ref, ob_ref, outw_ref,
    pg_ref, glng_ref, glnb_ref, gproj_ref, ggate_ref, gog_ref, gob_ref, gow_ref,
    xs, w_s, wo_s, vec_s, xf, wt_s, wot_s, gain_s, mask_s,
    hat_s, inv_s, nrm_s, la_s, ga_s, lb_s, gb_s, go_s,
    mhat_s, minv_s, mn_s, oc_s, up_s, dout_s, dpre_s, acc_s,
    scr_a, scr_b, lt_s, rt_s, dt_s,
    send_lr, recv_lr, send_m, recv_m, send_d, recv_d, send_g, recv_g,
    pgb, gs, recv_b, send_c, recv_c, recv_o,
    psend, precv, ssem, rsem, csem, dsem,
):
    m, r, c = lax.axis_index("section"), lax.axis_index("row"), lax.axis_index("col")
    me = r * COLS + c
    other = 1 - m
    partner = (other, r, c)

    barrier = pltpu.get_barrier_semaphore()

    def greet(k, carry):
        d = lax.rem(me + k, PEERS)
        pl.semaphore_signal(barrier, inc=1, device_id=(m, d // COLS, lax.rem(d, COLS)), device_id_type=MESH)
        return carry

    def greet_row(k, carry):
        pl.semaphore_signal(barrier, inc=1, device_id=(other, r, k), device_id_type=MESH)
        return carry

    lax.fori_loop(1, PEERS, greet, 0)
    lax.fori_loop(0, COLS, greet_row, 0)

    low = lax.broadcasted_iota(jnp.int32, (128, 128), 1) < 64
    low1 = lax.broadcasted_iota(jnp.int32, (8, 128), 1) < 64

    def exchange(src, dst, phase, sec):
        def send(k, carry):
            d = lax.rem(me + k, PEERS)
            pltpu.make_async_remote_copy(
                src.at[sec, d], dst.at[sec, me], ssem.at[phase, sec], rsem.at[phase, sec],
                device_id=(m, d // COLS, lax.rem(d, COLS)), device_id_type=MESH,
            ).start()
            return carry

        lax.fori_loop(1, PEERS, send, 0)
        dst[sec, me] = src[sec, me]

    def arrived(dst, phase, sec):
        part = dst.at[sec, pl.ds(0, PEERS - 1)]
        pltpu.make_async_copy(part, part, rsem.at[phase, sec]).wait()

    def sent(src, phase, sec):
        part = src.at[sec, pl.ds(0, PEERS - 1)]
        pltpu.make_async_copy(part, part, ssem.at[phase, sec]).wait()

    def lanes(b):
        return pl.ds(pl.multiple_of(b * WIDE, WIDE), WIDE)

    def cells_to_lanes(src, b):
        out = []
        for u in range(2):
            t = 2 * b + u
            rows = jnp.concatenate([src[pl.ds(t, 64, stride=16), :], src[pl.ds(t + 8, 64, stride=16), :]], axis=0)
            out.append(rows.T)
        return jnp.concatenate(out, axis=1)

    def lanes_to_cells(value, dst, b):
        for u in range(2):
            t = 2 * b + u
            rows = value[:, 128 * u:128 * u + 128].T
            dst[pl.ds(t, 64, stride=16), :] = rows[:64]
            dst[pl.ds(t + 8, 64, stride=16), :] = rows[64:]

    def spread(value, dst, b):
        for u in range(2):
            dst[pl.ds(2 * b + u, 128, stride=8), :] = value[:, 128 * u:128 * u + 128]

    def gathered(src, b):
        return jnp.concatenate([src[pl.ds(2 * b + u, 128, stride=8), :] for u in range(2)], axis=1)

    def wide(g):
        return jnp.concatenate([g, g], axis=1)

    whole = jnp.where(m == 0, mask_v[0:1, :], mask_v[1:2, :]).astype(F32)
    half = jnp.broadcast_to(jnp.where(r >= 2, whole[:, 128:], whole[:, :128]), (8, 128))
    turned = pltpu.roll(half, 64, 1)
    is_even = lax.rem(r, 2) == 0
    mask_i = jnp.where(low1, jnp.where(is_even, half, turned), jnp.where(is_even, turned, half))
    for t in range(8):
        first = mask_sm[m, c * 16 + t].astype(F32)
        second = mask_sm[m, c * 16 + 8 + t].astype(F32)
        mask_s[:, 128 * t:128 * t + 128] = mask_i * jnp.where(low1, first, second)

    def prepare(sec):
        wt_s[sec] = w_s[sec].astype(F32).T.astype(BF16)
        wot_s[sec] = wo_s[sec].astype(F32).T.astype(BF16)
        for v in range(4):
            gain_s[sec, v] = jnp.broadcast_to(vec_s[sec, v:v + 1, :], (128, 128)).T

    def front(sec):
        prepare(sec)
        xf[...] = xs[sec].astype(F32)

        def block(b, carry):
            at = lanes(b)
            x = cells_to_lanes(xf, b)
            centred = x - mean0(x)
            inv = lax.rsqrt(mean0(centred * centred) + EPSILON)
            hat = centred * inv
            nrm = (hat * wide(gain_s[sec, 0]) + wide(gain_s[sec, 1])).astype(BF16)
            hat_s[sec, :, at] = hat
            inv_s[sec, :, at] = jnp.broadcast_to(inv, (8, WIDE))
            nrm_s[sec, :, at] = nrm
            mask = mask_s[0:1, at]
            lin = dot(wt_s[sec, 0:128], nrm)
            gate = sigmoid(dot(wt_s[sec, 128:256], nrm))
            la_s[sec, :, at] = lin
            ga_s[sec, :, at] = gate
            spread(gate * lin * mask, scr_a, b)
            lin = dot(wt_s[sec, 256:384], nrm)
            gate = sigmoid(dot(wt_s[sec, 384:512], nrm))
            lb_s[sec, :, at] = lin
            gb_s[sec, :, at] = gate
            spread(gate * lin * mask, scr_b, b)
            go_s[sec, :, at] = sigmoid(dot(wt_s[sec, 512:640], nrm))
            return carry

        lax.fori_loop(0, 4, block, 0)
        send_lr[sec, :, 0:16, :] = scr_a[...].reshape(PEERS, 16, 128).astype(BF16)
        send_lr[sec, :, 16:32, :] = scr_b[...].reshape(PEERS, 16, 128).astype(BF16)

    def assemble(src, sec, at, dst, first):
        for q in range(2):
            even = src[sec, 32 * q:32 * q + 16, at:at + 16, :].astype(F32)
            odd = src[sec, 32 * q + 16:32 * q + 32, at:at + 16, :].astype(F32)
            for ch in range(2):
                a = even[:, 8 * ch:8 * ch + 8, :].reshape(128, 128)
                b = odd[:, 8 * ch:8 * ch + 8, :].reshape(128, 128)
                k0 = jnp.where(low, a, pltpu.roll(b, 64, 1)).reshape(16, 1, 8, 128)
                k1 = jnp.where(low, pltpu.roll(a, 64, 1), b).reshape(16, 1, 8, 128)
                full = jnp.concatenate([k0, k1], axis=1).reshape(256, 128)
                dst[first + ch, :, 128 * q:128 * q + 128] = full.astype(BF16)

    def take_apart(pair, dst, sec, at):
        for q in range(2):
            evens, odds = [], []
            for y in pair:
                y4 = y[:, 128 * q:128 * q + 128].reshape(16, 2, 8, 128)
                y0 = y4[:, 0].reshape(128, 128)
                y1 = y4[:, 1].reshape(128, 128)
                evens.append(jnp.where(low, y0, pltpu.roll(y1, 64, 1)).reshape(16, 8, 128))
                odds.append(jnp.where(low, pltpu.roll(y0, 64, 1), y1).reshape(16, 8, 128))
            dst[sec, 32 * q:32 * q + 16, at:at + 16, :] = jnp.concatenate(evens, axis=1).astype(BF16)
            dst[sec, 32 * q + 16:32 * q + 32, at:at + 16, :] = jnp.concatenate(odds, axis=1).astype(BF16)

    def mix(sec):
        arrived(recv_lr, LR, sec)
        assemble(recv_lr, sec, 0, lt_s, 2 * sec)
        assemble(recv_lr, sec, 16, rt_s, 2 * sec)
        pair = [dot(rt_s[2 * sec + ch], lt_s[2 * sec + ch], 0, 0) for ch in range(2)]
        take_apart(pair, send_m, sec, 0)
        exchange(send_m, recv_m, MIX, sec)

    def out_forward(sec):
        arrived(recv_m, MIX, sec)
        scr_a[...] = recv_m[sec].astype(F32).reshape(N, 128)

        def block(b, carry):
            at = lanes(b)
            x = gathered(scr_a, b)
            centred = x - mean0(x)
            inv = lax.rsqrt(mean0(centred * centred) + EPSILON)
            hat = centred * inv
            mn = (hat * wide(gain_s[sec, 2]) + wide(gain_s[sec, 3])).astype(BF16)
            mhat_s[sec, :, at] = hat
            minv_s[sec, :, at] = jnp.broadcast_to(inv, (8, WIDE))
            mn_s[sec, :, at] = mn
            gate = go_s[sec, :, at]
            oc_s[sec, :, at] = dot(wot_s[sec], mn) * gate * (1.0 - gate)
            return carry

        lax.fori_loop(0, 4, block, 0)

    def out_backward(sec):
        acc_s[2] = jnp.zeros((128, WIDE), F32)
        acc_s[3] = jnp.zeros((128, WIDE), F32)

        def block(b, carry):
            at = lanes(b)
            up = up_s[sec, :, at]
            dout = (up * go_s[sec, :, at]).astype(BF16)
            dout_s[:, at] = dout
            dpre_s[512:640, at] = (up * oc_s[sec, :, at]).astype(BF16)
            dn = dot(wo_s[sec], dout)
            hat = mhat_s[sec, :, at]
            acc_s[2] += dn * hat
            acc_s[3] += dn
            e = dn * wide(gain_s[sec, 2])
            d = (e - mean0(e) - hat * mean0(e * hat)) * minv_s[sec, 0:1, at]
            spread(d, scr_b, b)
            return carry

        lax.fori_loop(0, 4, block, 0)
        send_d[sec] = scr_b[...].reshape(PEERS, 16, 128).astype(BF16)
        exchange(send_d, recv_d, DMIX, sec)

    def products_back(sec):
        arrived(recv_d, DMIX, sec)
        assemble(recv_d, sec, 0, dt_s, 0)
        pair = [dot(rt_s[2 * sec + ch], dt_s[ch]) for ch in range(2)]
        take_apart(pair, send_g, sec, 0)
        pair = [dot(lt_s[2 * sec + ch], dt_s[ch], 1, 1) for ch in range(2)]
        take_apart(pair, send_g, sec, 16)
        exchange(send_g, recv_g, DLR, sec)

    def in_part(sec):
        acc_s[0] = jnp.zeros((128, WIDE), F32)
        acc_s[1] = jnp.zeros((128, WIDE), F32)
        arrived(recv_g, DLR, sec)
        scr_a[...] = recv_g[sec, :, 0:16, :].astype(F32).reshape(N, 128)
        scr_b[...] = recv_g[sec, :, 16:32, :].astype(F32).reshape(N, 128)

        def block(b, carry):
            at = lanes(b)
            mask = mask_s[0:1, at]
            gate = ga_s[sec, :, at]
            dg = gathered(scr_a, b) * gate * mask
            dpre_s[0:128, at] = dg.astype(BF16)
            dpre_s[128:256, at] = (dg * la_s[sec, :, at] * (1.0 - gate)).astype(BF16)
            gate = gb_s[sec, :, at]
            dg = gathered(scr_b, b) * gate * mask
            dpre_s[256:384, at] = dg.astype(BF16)
            dpre_s[384:512, at] = (dg * lb_s[sec, :, at] * (1.0 - gate)).astype(BF16)
            din = dot(w_s[sec], dpre_s[:, at])
            hat = hat_s[sec, :, at]
            acc_s[0] += din * hat
            acc_s[1] += din
            f = din * wide(gain_s[sec, 0])
            up = up_s[sec, :, at] + (f - mean0(f) - hat * mean0(f * hat)) * inv_s[sec, 0:1, at]
            if sec > 0:
                up_s[sec - 1, :, at] = up
            lanes_to_cells(up, pgb.at[sec], b)
            return carry

        lax.fori_loop(0, 4, block, 0)

    def weight_grads(sec):
        for o in range(5):
            g = dot(nrm_s[sec], dpre_s[128 * o:128 * o + 128, :], 1, 1)
            gs[sec, :, 8 * o:8 * o + 8, :] = g.reshape(COLS, 8, 128)
        for v in range(4):
            total = (acc_s[v, :, 0:128] + acc_s[v, :, 128:256]).T
            gs[sec, 0, 48 + v:49 + v, :] = jnp.sum(total, axis=0, keepdims=True)

    def out_weight_grads(sec):
        gs[sec, :, 40:48, :] = dot(mn_s[sec], dout_s[...], 1, 1).reshape(COLS, 8, 128)

    def scatter_grads(sec):
        def send(k, carry):
            d = lax.rem(c + k, COLS)

            @pl.when(jnp.logical_or(m != sec, k > 0))
            def _():
                pltpu.make_async_remote_copy(
                    gs.at[sec, d], recv_b.at[m * COLS + c], ssem.at[RS, sec], rsem.at[RS, 0],
                    device_id=(sec, r, d), device_id_type=MESH,
                ).start()

            return carry

        lax.fori_loop(0, COLS, send, 0)

        @pl.when(m == sec)
        def _():
            recv_b[sec * COLS + c] = gs[sec, c]

    xs[m] = act_ref[m]
    w_s[m, :, 0:512] = proj_ref[...]
    w_s[m, :, 512:640] = gatew_ref[...]
    wo_s[m] = outw_ref[...]
    vec_s[m, 0:1] = lng_ref[...]
    vec_s[m, 1:2] = lnb_ref[...]
    vec_s[m, 2:3] = og_ref[...]
    vec_s[m, 3:4] = ob_ref[...]
    vec_s[m, 4:8] = jnp.zeros((4, 128), F32)
    for sec in range(2):
        gs[sec, :, 48:56, :] = jnp.zeros((COLS, 8, 128), F32)

    front(m)
    pl.semaphore_wait(barrier, PEERS - 1 + COLS)
    swaps = [
        pltpu.make_async_remote_copy(
            src, dst, psend.at[n], precv.at[n], device_id=partner, device_id_type=MESH
        )
        for n, (src, dst) in enumerate(
            [(act_ref.at[other], xs.at[m]), (w_s.at[m], w_s.at[m]), (wo_s.at[m], wo_s.at[m]), (vec_s.at[m], vec_s.at[m])]
        )
    ]
    for swap in swaps:
        swap.start()
    exchange(send_lr, recv_lr, LR, m)

    def turn(b, carry):
        up_s[1, :, lanes(b)] = cells_to_lanes(cot_ref.at[m], b)
        return carry

    lax.fori_loop(0, 4, turn, 0)
    for swap in swaps:
        swap.wait_recv()
    front(other)
    exchange(send_lr, recv_lr, LR, other)

    mix(m)
    mix(other)
    out_forward(1)
    out_backward(1)
    out_forward(0)
    out_weight_grads(1)
    products_back(1)
    in_part(1)
    weight_grads(1)
    out_backward(0)
    scatter_grads(1)
    out_weight_grads(0)
    products_back(0)
    in_part(0)
    handed = pltpu.make_async_remote_copy(
        pgb.at[other], pg_ref.at[m], psend.at[PG_COPY], precv.at[PG_COPY], device_id=partner, device_id_type=MESH
    )
    handed.start()
    weight_grads(0)
    scatter_grads(0)
    pg_ref[m] = pgb[m]

    part = recv_b.at[pl.ds(0, 2 * COLS - 1)]
    pltpu.make_async_copy(part, part, rsem.at[RS, 0]).wait()
    total = jnp.sum(recv_b[...], axis=0)
    send_c[...] = total
    recv_c[r] = total
    for k in range(1, ROWS):
        pltpu.make_async_remote_copy(
            send_c, recv_c.at[r], csem.at[0], csem.at[1],
            device_id=(m, lax.rem(r + k, ROWS), c), device_id_type=MESH,
        ).start()
    part = recv_c.at[pl.ds(0, ROWS - 1)]
    pltpu.make_async_copy(part, part, csem.at[1]).wait()
    recv_o[c] = jnp.sum(recv_c[...], axis=0)

    def give(k, carry):
        pltpu.make_async_remote_copy(
            recv_o.at[c], recv_o.at[c], dsem.at[0], dsem.at[1],
            device_id=(m, r, lax.rem(c + k, COLS)), device_id_type=MESH,
        ).start()
        return carry

    lax.fori_loop(1, COLS, give, 0)
    for src, phase in ((send_lr, LR), (send_m, MIX), (send_d, DMIX), (send_g, DLR)):
        for sec in range(2):
            sent(src, phase, sec)
    for sec in range(2):
        part = gs.at[sec, pl.ds(0, COLS - 1)]
        pltpu.make_async_copy(part, part, ssem.at[RS, sec]).wait()

        @pl.when(m != sec)
        def _():
            part = gs.at[sec, 0]
            pltpu.make_async_copy(part, part, ssem.at[RS, sec]).wait()

    part = recv_c.at[pl.ds(0, ROWS - 1)]
    pltpu.make_async_copy(part, part, csem.at[0]).wait()
    for swap in swaps:
        swap.wait_send()
    part = recv_o.at[pl.ds(0, COLS - 1)]
    pltpu.make_async_copy(part, part, dsem.at[0]).wait()
    pltpu.make_async_copy(part, part, dsem.at[1]).wait()
    for o in range(4):
        gproj_ref[:, 128 * o:128 * o + 128] = recv_o[:, 8 * o:8 * o + 8, :].reshape(128, 128)
    ggate_ref[...] = recv_o[:, 32:40, :].reshape(128, 128)
    gow_ref[...] = recv_o[:, 40:48, :].reshape(128, 128)
    glng_ref[...] = recv_o[0, 48:49, :]
    glnb_ref[...] = recv_o[0, 49:50, :]
    gog_ref[...] = recv_o[0, 50:51, :]
    gob_ref[...] = recv_o[0, 51:52, :]
    handed.wait()


def on_device(act, cot, mask, lng, lnb, proj, gatew, og, ob, outw):
    vmem = pl.BlockSpec(memory_space=pltpu.VMEM)
    smem = pl.BlockSpec(memory_space=pltpu.SMEM)

    def v(shape, dtype=F32):
        return pltpu.VMEM(shape, dtype)

    sds = jax.ShapeDtypeStruct
    results = pl.pallas_call(
        kernel,
        out_shape=(
            sds((2, N, 128), F32), sds((1, 128), F32), sds((1, 128), F32), sds((128, 512), F32),
            sds((128, 128), F32), sds((1, 128), F32), sds((1, 128), F32), sds((128, 128), F32),
        ),
        in_specs=[vmem, vmem, vmem, smem] + [vmem] * 7,
        out_specs=(vmem,) * 8,
        scratch_shapes=[
            v((2, N, 128), BF16), v((2, 128, 640), BF16), v((2, 128, 128), BF16), v((2, 8, 128)), v((N, 128)),
            v((2, 640, 128), BF16), v((2, 128, 128), BF16), v((2, 4, 128, 128)), v((8, N)),
            v((2, 128, N)), v((2, 8, N)), v((2, 128, N), BF16),
            v((2, 128, N)), v((2, 128, N)), v((2, 128, N)), v((2, 128, N)), v((2, 128, N)),
            v((2, 128, N)), v((2, 8, N)), v((2, 128, N), BF16), v((2, 128, N)), v((2, 128, N)),
            v((128, N), BF16), v((640, N), BF16), v((4, 128, WIDE)),
            v((N, 128)), v((N, 128)), v((4, 256, 256), BF16), v((4, 256, 256), BF16), v((2, 256, 256), BF16),
            v((2, PEERS, 32, 128), BF16), v((2, PEERS, 32, 128), BF16),
            v((2, PEERS, 16, 128), BF16), v((2, PEERS, 16, 128), BF16),
            v((2, PEERS, 16, 128), BF16), v((2, PEERS, 16, 128), BF16),
            v((2, PEERS, 32, 128), BF16), v((2, PEERS, 32, 128), BF16),
            v((2, N, 128)), v((2, COLS, 56, 128)), v((2 * COLS, 56, 128)),
            v((56, 128)), v((ROWS, 56, 128)), v((COLS, 56, 128)),
            pltpu.SemaphoreType.DMA((5,)), pltpu.SemaphoreType.DMA((5,)),
            pltpu.SemaphoreType.DMA((5, 2)), pltpu.SemaphoreType.DMA((5, 2)),
            pltpu.SemaphoreType.DMA((2,)), pltpu.SemaphoreType.DMA((2,)),
        ],
        compiler_params=pltpu.CompilerParams(
            collective_id=1, has_side_effects=True, vmem_limit_bytes=56 * 2**20
        ),
    )(
        act.reshape(2, N, 128), cot.reshape(2, N, 128), mask, mask, lng, lnb, proj[0], gatew[0], og, ob, outw[0]
    )
    pg, glng, glnb, gproj, ggate, gog, gob, gow = results
    return (
        pg.reshape(1, 2, 64, 16, 128), glng, glnb, gproj[None], ggate[None], gog, gob, gow[None],
    )


def solution(mesh):
    vector, matrix = P("section", None), P("section", None, None)
    grid = P("section", None, "row", "col", None)
    return jax.shard_map(
        on_device,
        mesh=mesh,
        in_specs=(grid, P(None, "row", "col", None), P(), vector, vector, matrix, matrix, vector, vector, matrix),
        out_specs=(grid, vector, vector, matrix, matrix, vector, vector, matrix),
        check_vma=False,
    )
```

```python
import jax
import jax.numpy as jnp
from jax import lax
from jax.experimental import pallas as pl
from jax.experimental.pallas import tpu as pltpu
from jax.sharding import PartitionSpec as P

EPSILON = 1e-05
MESH = pl.DeviceIdType.MESH
F32 = jnp.float32
BF16 = jnp.bfloat16
ROWS = 4
COLS = 16
PEERS = ROWS * COLS
N = 1024
WIDE = 256

X_COPY, W_COPY, O_COPY, V_COPY, PG_COPY = range(5)
LR, MIX, DMIX, DLR, RS = range(5)
OWNERS = 49


def sigmoid(v):
    return 0.5 * jnp.tanh(0.5 * v) + 0.5


def mean0(v):
    return jnp.mean(v, axis=0, keepdims=True)


def dot(a, b, ca=1, cb=0):
    return lax.dot_general(a, b, (((ca,), (cb,)), ((), ())), preferred_element_type=F32)


def kernel(
    act_ref, cot_ref, mask_v, mask_sm, lng_ref, lnb_ref, proj_ref, gatew_ref, og_ref, ob_ref, outw_ref,
    pg_ref, recv_o,
    xs, w_s, wo_s, vec_s, xf, wt_s, wot_s, gain_s, mask_s,
    hat_s, inv_s, nrm_s, la_s, ga_s, lb_s, gb_s, go_s,
    mhat_s, minv_s, mn_s, oc_s, up_s, dout_s, dpre_s, acc_s,
    scr_a, scr_b, lt_s, rt_s, dt_s,
    send_lr, recv_lr, send_m, recv_m, send_d, recv_d, send_g, recv_g,
    pgb, gs, recv_b,
    psend, precv, ssem, rsem, dsem,
):
    m, r, c = lax.axis_index("section"), lax.axis_index("row"), lax.axis_index("col")
    me = r * COLS + c
    other = 1 - m
    partner = (other, r, c)

    z, y = c // 4, lax.rem(c, 4)

    def step4(v):
        return jnp.where(v == 0, 2, jnp.where(v == 3, 0, 2 * v - 1))

    def peer(k):
        to_r = lax.rem(r + step4(lax.rem(k, 4)), 4)
        to_c = lax.rem(z + step4(k // 16), 4) * 4 + lax.rem(y + step4(lax.rem(k // 4, 4)), 4)
        return to_r, to_c, to_r * COLS + to_c

    barrier = pltpu.get_barrier_semaphore()

    def greet(k, carry):
        to_r, to_c, _ = peer(k)
        pl.semaphore_signal(barrier, inc=1, device_id=(other, to_r, to_c), device_id_type=MESH)

        @pl.when(k < PEERS - 1)
        def _():
            pl.semaphore_signal(barrier, inc=1, device_id=(m, to_r, to_c), device_id_type=MESH)

        return carry

    lax.fori_loop(0, PEERS, greet, 0)

    low = lax.broadcasted_iota(jnp.int32, (128, 128), 1) < 64
    low1 = lax.broadcasted_iota(jnp.int32, (8, 128), 1) < 64

    def exchange(src, dst, phase, sec):
        def send(k, carry):
            to_r, to_c, d = peer(k)
            pltpu.make_async_remote_copy(
                src.at[sec, d], dst.at[sec, me], ssem.at[phase, sec], rsem.at[phase, sec],
                device_id=(m, to_r, to_c), device_id_type=MESH,
            ).start()
            return carry

        lax.fori_loop(0, PEERS - 1, send, 0)
        dst[sec, me] = src[sec, me]

    def exchange_lr():
        def send(k, carry):
            to_r, to_c, d = peer(k)
            for dest in (m, other):
                def start(dest=dest):
                    pltpu.make_async_remote_copy(
                        send_lr.at[dest, d], recv_lr.at[m, me], ssem.at[LR, dest], rsem.at[LR, m],
                        device_id=(dest, to_r, to_c), device_id_type=MESH,
                    ).start()

                if dest is m:
                    pl.when(k < PEERS - 1)(start)
                else:
                    start()
            return carry

        lax.fori_loop(0, PEERS, send, 0)
        recv_lr[m, me] = send_lr[m, me]

    def arrived_lr(sec):
        @pl.when(m == sec)
        def _():
            arrived(recv_lr, LR, sec)

        @pl.when(m != sec)
        def _():
            part = recv_lr.at[sec]
            pltpu.make_async_copy(part, part, rsem.at[LR, sec]).wait()


    def arrived(dst, phase, sec):
        part = dst.at[sec, pl.ds(0, PEERS - 1)]
        pltpu.make_async_copy(part, part, rsem.at[phase, sec]).wait()

    def sent(src, phase, sec):
        part = src.at[sec, pl.ds(0, PEERS - 1)]
        pltpu.make_async_copy(part, part, ssem.at[phase, sec]).wait()

    def lanes(b):
        return pl.ds(pl.multiple_of(b * WIDE, WIDE), WIDE)

    def cells_to_lanes(src, b):
        out = []
        for u in range(2):
            t = 2 * b + u
            rows = jnp.concatenate([src[pl.ds(t, 64, stride=16), :], src[pl.ds(t + 8, 64, stride=16), :]], axis=0)
            out.append(rows.T)
        return jnp.concatenate(out, axis=1)

    def lanes_to_cells(value, dst, b):
        for u in range(2):
            t = 2 * b + u
            rows = value[:, 128 * u:128 * u + 128].T
            dst[pl.ds(t, 64, stride=16), :] = rows[:64]
            dst[pl.ds(t + 8, 64, stride=16), :] = rows[64:]

    def spread(value, dst, b):
        for u in range(2):
            dst[pl.ds(2 * b + u, 128, stride=8), :] = value[:, 128 * u:128 * u + 128]

    def gathered(src, b):
        return jnp.concatenate([src[pl.ds(2 * b + u, 128, stride=8), :] for u in range(2)], axis=1)

    def wide(g):
        return jnp.concatenate([g, g], axis=1)

    is_even = lax.rem(r, 2) == 0
    for n in range(2):
        whole = mask_v[n:n + 1, :].astype(F32)
        half = jnp.broadcast_to(jnp.where(r >= 2, whole[:, 128:], whole[:, :128]), (8, 128))
        turned = pltpu.roll(half, 64, 1)
        mask_i = jnp.where(low1, jnp.where(is_even, half, turned), jnp.where(is_even, turned, half))
        for t in range(8):
            first = mask_sm[n, c * 16 + t].astype(F32)
            second = mask_sm[n, c * 16 + 8 + t].astype(F32)
            mask_s[n, :, 128 * t:128 * t + 128] = mask_i * jnp.where(low1, first, second)

    def prepare(sec):
        wt_s[sec] = w_s[sec].astype(F32).T.astype(BF16)
        wot_s[sec] = wo_s[sec].astype(F32).T.astype(BF16)
        for v in range(4):
            gain_s[sec, v] = jnp.broadcast_to(vec_s[sec, v:v + 1, :], (128, 128)).T

    def front(sec, source, save, target):
        xf[...] = source[...].astype(F32)

        def block(b, carry):
            at = lanes(b)
            x = cells_to_lanes(xf, b)
            centred = x - mean0(x)
            inv = lax.rsqrt(mean0(centred * centred) + EPSILON)
            hat = centred * inv
            nrm = (hat * wide(gain_s[sec, 0]) + wide(gain_s[sec, 1])).astype(BF16)
            lin_a = dot(wt_s[sec, 0:128], nrm)
            gate_a = sigmoid(dot(wt_s[sec, 128:256], nrm))
            lin_b = dot(wt_s[sec, 256:384], nrm)
            gate_b = sigmoid(dot(wt_s[sec, 384:512], nrm))
            if target is not None:
                mask = mask_s[target, 0:1, at]
                spread(gate_a * lin_a * mask, scr_a, b)
                spread(gate_b * lin_b * mask, scr_b, b)
            if save:
                hat_s[sec, :, at] = hat
                inv_s[sec, :, at] = jnp.broadcast_to(inv, (8, WIDE))
                nrm_s[sec, :, at] = nrm
                la_s[sec, :, at] = lin_a
                ga_s[sec, :, at] = gate_a
                lb_s[sec, :, at] = lin_b
                gb_s[sec, :, at] = gate_b
                go_s[sec, :, at] = sigmoid(dot(wt_s[sec, 512:640], nrm))
            return carry

        lax.fori_loop(0, 4, block, 0)
        if target is not None:
            send_lr[target, :, 0:16, :] = scr_a[...].reshape(PEERS, 16, 128).astype(BF16)
            send_lr[target, :, 16:32, :] = scr_b[...].reshape(PEERS, 16, 128).astype(BF16)

    def assemble(src, sec, at, dst, first):
        for q in range(2):
            even = src[sec, 32 * q:32 * q + 16, at:at + 16, :].astype(F32)
            odd = src[sec, 32 * q + 16:32 * q + 32, at:at + 16, :].astype(F32)
            for ch in range(2):
                a = even[:, 8 * ch:8 * ch + 8, :].reshape(128, 128)
                b = odd[:, 8 * ch:8 * ch + 8, :].reshape(128, 128)
                k0 = jnp.where(low, a, pltpu.roll(b, 64, 1)).reshape(16, 1, 8, 128)
                k1 = jnp.where(low, pltpu.roll(a, 64, 1), b).reshape(16, 1, 8, 128)
                full = jnp.concatenate([k0, k1], axis=1).reshape(256, 128)
                dst[first + ch, :, 128 * q:128 * q + 128] = full.astype(BF16)

    def take_apart(pair, dst, sec, at):
        for q in range(2):
            evens, odds = [], []
            for y in pair:
                y4 = y[:, 128 * q:128 * q + 128].reshape(16, 2, 8, 128)
                y0 = y4[:, 0].reshape(128, 128)
                y1 = y4[:, 1].reshape(128, 128)
                evens.append(jnp.where(low, y0, pltpu.roll(y1, 64, 1)).reshape(16, 8, 128))
                odds.append(jnp.where(low, pltpu.roll(y0, 64, 1), y1).reshape(16, 8, 128))
            dst[sec, 32 * q:32 * q + 16, at:at + 16, :] = jnp.concatenate(evens, axis=1).astype(BF16)
            dst[sec, 32 * q + 16:32 * q + 32, at:at + 16, :] = jnp.concatenate(odds, axis=1).astype(BF16)

    def mix(sec):
        arrived_lr(sec)
        assemble(recv_lr, sec, 0, lt_s, 2 * sec)
        assemble(recv_lr, sec, 16, rt_s, 2 * sec)
        pair = [dot(rt_s[2 * sec + ch], lt_s[2 * sec + ch], 0, 0) for ch in range(2)]
        take_apart(pair, send_m, sec, 0)
        exchange(send_m, recv_m, MIX, sec)

    def out_forward(sec):
        arrived(recv_m, MIX, sec)
        scr_a[...] = recv_m[sec].astype(F32).reshape(N, 128)

        def block(b, carry):
            at = lanes(b)
            x = gathered(scr_a, b)
            centred = x - mean0(x)
            inv = lax.rsqrt(mean0(centred * centred) + EPSILON)
            hat = centred * inv
            mn = (hat * wide(gain_s[sec, 2]) + wide(gain_s[sec, 3])).astype(BF16)
            mhat_s[sec, :, at] = hat
            minv_s[sec, :, at] = jnp.broadcast_to(inv, (8, WIDE))
            mn_s[sec, :, at] = mn
            gate = go_s[sec, :, at]
            oc_s[sec, :, at] = dot(wot_s[sec], mn) * gate * (1.0 - gate)
            return carry

        lax.fori_loop(0, 4, block, 0)

    def out_backward(sec):
        acc_s[sec, 2] = jnp.zeros((128, WIDE), F32)
        acc_s[sec, 3] = jnp.zeros((128, WIDE), F32)

        def block(b, carry):
            at = lanes(b)
            up = up_s[sec, :, at]
            dout = (up * go_s[sec, :, at]).astype(BF16)
            dout_s[sec, :, at] = dout
            dpre_s[sec, 512:640, at] = (up * oc_s[sec, :, at]).astype(BF16)
            dn = dot(wo_s[sec], dout)
            hat = mhat_s[sec, :, at]
            acc_s[sec, 2] += dn * hat
            acc_s[sec, 3] += dn
            e = dn * wide(gain_s[sec, 2])
            d = (e - mean0(e) - hat * mean0(e * hat)) * minv_s[sec, 0:1, at]
            spread(d, scr_b, b)
            return carry

        lax.fori_loop(0, 4, block, 0)
        send_d[sec] = scr_b[...].reshape(PEERS, 16, 128).astype(BF16)
        exchange(send_d, recv_d, DMIX, sec)

    def products_back(sec):
        arrived(recv_d, DMIX, sec)
        assemble(recv_d, sec, 0, dt_s, 0)
        pair = [dot(rt_s[2 * sec + ch], dt_s[ch]) for ch in range(2)]
        take_apart(pair, send_g, sec, 0)
        pair = [dot(lt_s[2 * sec + ch], dt_s[ch], 1, 1) for ch in range(2)]
        take_apart(pair, send_g, sec, 16)
        exchange(send_g, recv_g, DLR, sec)

    def in_part(sec):
        acc_s[sec, 0] = jnp.zeros((128, WIDE), F32)
        acc_s[sec, 1] = jnp.zeros((128, WIDE), F32)
        arrived(recv_g, DLR, sec)
        scr_a[...] = recv_g[sec, :, 0:16, :].astype(F32).reshape(N, 128)
        scr_b[...] = recv_g[sec, :, 16:32, :].astype(F32).reshape(N, 128)

        def block(b, carry):
            at = lanes(b)
            mask = mask_s[m, 0:1, at]
            gate = ga_s[sec, :, at]
            dg = gathered(scr_a, b) * gate * mask
            dpre_s[sec, 0:128, at] = dg.astype(BF16)
            dpre_s[sec, 128:256, at] = (dg * la_s[sec, :, at] * (1.0 - gate)).astype(BF16)
            gate = gb_s[sec, :, at]
            dg = gathered(scr_b, b) * gate * mask
            dpre_s[sec, 256:384, at] = dg.astype(BF16)
            dpre_s[sec, 384:512, at] = (dg * lb_s[sec, :, at] * (1.0 - gate)).astype(BF16)
            din = dot(w_s[sec], dpre_s[sec, :, at])
            hat = hat_s[sec, :, at]
            acc_s[sec, 0] += din * hat
            acc_s[sec, 1] += din
            f = din * wide(gain_s[sec, 0])
            up = up_s[sec, :, at] + (f - mean0(f) - hat * mean0(f * hat)) * inv_s[sec, 0:1, at]
            up_s[sec - 1 if sec > 0 else 2, :, at] = up
            return carry

        lax.fori_loop(0, 4, block, 0)

    def back_to_cells(sec):
        def block(b, carry):
            lanes_to_cells(up_s[sec - 1 if sec > 0 else 2, :, lanes(b)], pgb.at[sec], b)
            return carry

        lax.fori_loop(0, 4, block, 0)

    def early_grads(sec):
        g = dot(nrm_s[sec], dpre_s[sec, 512:640, :], 1, 1)
        gs[sec, 32:40] = g.reshape(8, 16, 128).astype(BF16)
        g = dot(mn_s[sec], dout_s[sec], 1, 1)
        gs[sec, 40:48] = g.reshape(8, 16, 128).astype(BF16)
        scatter_grads(sec, True)

    def late_grads(sec):
        for o in range(4):
            g = dot(nrm_s[sec], dpre_s[sec, 128 * o:128 * o + 128, :], 1, 1)
            gs[sec, 8 * o:8 * o + 8] = g.reshape(8, 16, 128).astype(BF16)
        rows = []
        for v in range(4):
            total = (acc_s[sec, v, :, 0:128] + acc_s[sec, v, :, 128:256]).T
            rows.append(jnp.sum(total, axis=0, keepdims=True))
        rows = jnp.concatenate(rows + [jnp.zeros((4, 128), F32)], axis=0)
        high = rows.astype(BF16).astype(F32)
        gs[sec, 48] = jnp.concatenate([high, rows - high], axis=0).astype(BF16)
        scatter_grads(sec, False)

    def scatter_grads(sec, early):
        def send(k, carry):
            to_r, to_c, d = peer(k)
            in_early = jnp.logical_and(d >= 32, d < 48)
            wanted = in_early if early else jnp.logical_and(d < OWNERS, jnp.logical_not(in_early))
            away = jnp.logical_or(m != sec, k < PEERS - 1)

            @pl.when(jnp.logical_and(wanted, away))
            def _():
                pltpu.make_async_remote_copy(
                    gs.at[sec, d], recv_b.at[m * PEERS + me], ssem.at[RS, sec], rsem.at[RS, 0],
                    device_id=(sec, to_r, to_c), device_id_type=MESH,
                ).start()

            @pl.when(jnp.logical_and(wanted, jnp.logical_not(away)))
            def _():
                recv_b[m * PEERS + me] = gs[sec, d]

            return carry

        lax.fori_loop(0, PEERS, send, 0)

    def gather_grads():
        @pl.when(me < OWNERS)
        def _():
            part = recv_b.at[pl.ds(0, 2 * PEERS - 1)]
            pltpu.make_async_copy(part, part, rsem.at[RS, 0]).wait()
            recv_o[me] = jnp.sum(recv_b[...].astype(F32), axis=0)

            def give(k, carry):
                to_r, to_c, _ = peer(k)
                pltpu.make_async_remote_copy(
                    recv_o.at[me], recv_o.at[me], dsem.at[0], dsem.at[1],
                    device_id=(m, to_r, to_c), device_id_type=MESH,
                ).start()
                return carry

            lax.fori_loop(0, PEERS - 1, give, 0)

    xs[m] = act_ref[m]
    w_s[m, :, 0:512] = proj_ref[...]
    w_s[m, :, 512:640] = gatew_ref[...]
    wo_s[m] = outw_ref[...]
    vec_s[m, 0:1] = lng_ref[...]
    vec_s[m, 1:2] = lnb_ref[...]
    vec_s[m, 2:3] = og_ref[...]
    vec_s[m, 3:4] = ob_ref[...]
    vec_s[m, 4:8] = jnp.zeros((4, 128), F32)

    prepare(m)
    front(m, act_ref.at[m], True, m)
    front(m, act_ref.at[other], False, other)
    pl.semaphore_wait(barrier, 2 * PEERS - 1)

    @pl.when(m == 1)
    def _():
        exchange_lr()

    swaps = [
        pltpu.make_async_remote_copy(
            src, dst, psend.at[n], precv.at[n], device_id=partner, device_id_type=MESH
        )
        for n, (src, dst) in enumerate(
            [(act_ref.at[other], xs.at[m]), (w_s.at[m], w_s.at[m]), (wo_s.at[m], wo_s.at[m]), (vec_s.at[m], vec_s.at[m])]
        )
    ]
    for swap in swaps:
        swap.start()

    def turn(b, carry):
        up_s[1, :, lanes(b)] = cells_to_lanes(cot_ref.at[m], b)
        return carry

    lax.fori_loop(0, 4, turn, 0)
    for swap in swaps:
        swap.wait_recv()
    prepare(other)
    front(other, xs.at[other], True, None)

    mix(1)

    @pl.when(m == 0)
    def _():
        exchange_lr()

    out_forward(1)
    out_backward(1)
    mix(0)
    early_grads(1)
    products_back(1)
    out_forward(0)
    in_part(1)
    out_backward(0)
    late_grads(1)
    back_to_cells(1)
    handed = pltpu.make_async_remote_copy(
        pgb.at[other], pg_ref.at[m], psend.at[PG_COPY], precv.at[PG_COPY], device_id=partner, device_id_type=MESH
    )

    @pl.when(m == 0)
    def _():
        handed.start()

    @pl.when(m == 1)
    def _():
        pg_ref[1] = pgb[1]

    products_back(0)
    early_grads(0)

    @pl.when(m == 1)
    def _():
        gather_grads()

    in_part(0)
    late_grads(0)
    back_to_cells(0)

    @pl.when(m == 1)
    def _():
        handed.start()

    @pl.when(m == 0)
    def _():
        pg_ref[0] = pgb[0]
        gather_grads()

    for src, phase in ((send_m, MIX), (send_d, DMIX), (send_g, DLR)):
        for sec in range(2):
            sent(src, phase, sec)
    sent(send_lr, LR, m)
    part = send_lr.at[other]
    pltpu.make_async_copy(part, part, ssem.at[LR, other]).wait()
    for sec in range(2):
        own_rows = jnp.logical_and(m == sec, me < OWNERS)
        for count, which in ((OWNERS - 1, own_rows), (OWNERS, jnp.logical_not(own_rows))):

            @pl.when(which)
            def _(count=count, sec=sec):
                part = gs.at[sec, pl.ds(0, count)]
                pltpu.make_async_copy(part, part, ssem.at[RS, sec]).wait()

    for swap in swaps:
        swap.wait_send()
    handed.wait()

    @pl.when(me >= OWNERS)
    def _():
        part = recv_o.at[pl.ds(0, OWNERS)]
        pltpu.make_async_copy(part, part, dsem.at[1]).wait()

    @pl.when(me < OWNERS)
    def _():
        part = recv_o.at[pl.ds(0, OWNERS - 1)]
        pltpu.make_async_copy(part, part, dsem.at[1]).wait()
        part = recv_o.at[pl.ds(0, PEERS - 1)]
        pltpu.make_async_copy(part, part, dsem.at[0]).wait()


def write_out(pg_in, o_ref, pg_ref, glng_ref, glnb_ref, gproj_ref, ggate_ref, gog_ref, gob_ref, gow_ref, held, sem_in, sem_out):
    parts = [pl.ds(n * 256, 256) for n in range(8)]
    come = [pltpu.make_async_copy(pg_in.at[p], held.at[p], sem_in.at[n]) for n, p in enumerate(parts)]
    go = [pltpu.make_async_copy(held.at[p], pg_ref.at[p], sem_out.at[n]) for n, p in enumerate(parts)]
    for copy in come:
        copy.start()
    for o in range(4):
        gproj_ref[:, 128 * o:128 * o + 128] = o_ref[8 * o:8 * o + 8].reshape(128, 128)
    ggate_ref[...] = o_ref[32:40].reshape(128, 128)
    gow_ref[...] = o_ref[40:48].reshape(128, 128)
    for v, ref in enumerate((glng_ref, glnb_ref, gog_ref, gob_ref)):
        ref[...] = o_ref[48, v:v + 1, :] + o_ref[48, 8 + v:9 + v, :]
    for copy_in, copy_out in zip(come, go):
        copy_in.wait()
        copy_out.start()
    for copy in go:
        copy.wait()


def on_device(act, cot, mask, lng, lnb, proj, gatew, og, ob, outw):
    vmem = pl.BlockSpec(memory_space=pltpu.VMEM)
    smem = pl.BlockSpec(memory_space=pltpu.SMEM)

    def v(shape, dtype=F32):
        return pltpu.VMEM(shape, dtype)

    sds = jax.ShapeDtypeStruct
    pg, rows = pl.pallas_call(
        kernel,
        out_shape=(sds((2, N, 128), F32), sds((PEERS, 16, 128), F32)),
        in_specs=[vmem, vmem, vmem, smem] + [vmem] * 7,
        out_specs=(vmem,) * 2,
        scratch_shapes=[
            v((2, N, 128), BF16), v((2, 128, 640), BF16), v((2, 128, 128), BF16), v((2, 8, 128)), v((N, 128)),
            v((2, 640, 128), BF16), v((2, 128, 128), BF16), v((2, 4, 128, 128)), v((2, 8, N)),
            v((2, 128, N)), v((2, 8, N)), v((2, 128, N), BF16),
            v((2, 128, N)), v((2, 128, N)), v((2, 128, N)), v((2, 128, N)), v((2, 128, N)),
            v((2, 128, N)), v((2, 8, N)), v((2, 128, N), BF16), v((2, 128, N)), v((3, 128, N)),
            v((2, 128, N), BF16), v((2, 640, N), BF16), v((2, 4, 128, WIDE)),
            v((N, 128)), v((N, 128)), v((4, 256, 256), BF16), v((4, 256, 256), BF16), v((2, 256, 256), BF16),
            v((2, PEERS, 32, 128), BF16), v((2, PEERS, 32, 128), BF16),
            v((2, PEERS, 16, 128), BF16), v((2, PEERS, 16, 128), BF16),
            v((2, PEERS, 16, 128), BF16), v((2, PEERS, 16, 128), BF16),
            v((2, PEERS, 32, 128), BF16), v((2, PEERS, 32, 128), BF16),
            v((2, N, 128)), v((2, OWNERS, 16, 128), BF16), v((2 * PEERS, 16, 128), BF16),
            pltpu.SemaphoreType.DMA((5,)), pltpu.SemaphoreType.DMA((5,)),
            pltpu.SemaphoreType.DMA((5, 2)), pltpu.SemaphoreType.DMA((5, 2)),
            pltpu.SemaphoreType.DMA((2,)),
        ],
        compiler_params=pltpu.CompilerParams(
            collective_id=1, has_side_effects=True, vmem_limit_bytes=56 * 2**20
        ),
    )(
        act.reshape(2, N, 128), cot.reshape(2, N, 128), mask, mask, lng, lnb, proj[0], gatew[0], og, ob, outw[0]
    )
    anywhere = pl.BlockSpec(memory_space=pl.ANY)
    pg, glng, glnb, gproj, ggate, gog, gob, gow = pl.pallas_call(
        write_out,
        out_shape=(
            sds((2 * N, 128), F32), sds((1, 128), F32), sds((1, 128), F32), sds((128, 512), F32),
            sds((128, 128), F32), sds((1, 128), F32), sds((1, 128), F32), sds((128, 128), F32),
        ),
        in_specs=[anywhere, vmem],
        out_specs=(anywhere,) + (vmem,) * 7,
        scratch_shapes=[v((2 * N, 128)), pltpu.SemaphoreType.DMA((8,)), pltpu.SemaphoreType.DMA((8,))],
    )(pg.reshape(2 * N, 128), rows)
    return (
        pg.reshape(1, 2, 64, 16, 128), glng, glnb, gproj[None], ggate[None], gog, gob, gow[None],
    )


def solution(mesh):
    vector, matrix = P("section", None), P("section", None, None)
    grid = P("section", None, "row", "col", None)
    return jax.shard_map(
        on_device,
        mesh=mesh,
        in_specs=(grid, P(None, "row", "col", None), P(), vector, vector, matrix, matrix, vector, vector, matrix),
        out_specs=(grid, vector, vector, matrix, matrix, vector, vector, matrix),
        check_vma=False,
    )
```

```python
import jax
import jax.numpy as jnp
from jax import lax
from jax.experimental import pallas as pl
from jax.experimental.pallas import tpu as pltpu
from jax.sharding import PartitionSpec as P

EPSILON = 1e-05
MESH = pl.DeviceIdType.MESH
F32 = jnp.float32
BF16 = jnp.bfloat16
ROWS = 4
COLS = 16
PEERS = ROWS * COLS
N = 1024
WIDE = 256

X_COPY, W_COPY, O_COPY, V_COPY, PG_COPY = range(5)
LR, MIX, DMIX, DLR, RS = range(5)
OWNERS = 49


def sigmoid(v):
    return 0.5 * jnp.tanh(0.5 * v) + 0.5


def mean0(v):
    return jnp.mean(v, axis=0, keepdims=True)


def dot(a, b, ca=1, cb=0):
    return lax.dot_general(a, b, (((ca,), (cb,)), ((), ())), preferred_element_type=F32)


def kernel(
    act_ref, cot_ref, mask_ref, lng_ref, lnb_ref, proj_ref, gatew_ref, og_ref, ob_ref, outw_ref,
    pg_ref, recv_o,
    act_s, cot_s, mask_v, mask_sm, xs, w_s, wo_s, vec_s, xf, wt_s, wot_s, gain_s, mask_s,
    hat_s, inv_s, nrm_s, la_s, ga_s, lb_s, gb_s, go_s,
    mhat_s, minv_s, mn_s, oc_s, up_s, dout_s, dpre_s, acc_s,
    dn_s, scr_a, scr_b, lt_s, rt_s, dt_s,
    send_lr, recv_lr, send_m, recv_m, send_d, recv_d, send_g, recv_g,
    pgb, gs, recv_b,
    isem, psend, precv, ssem, rsem, dsem,
):
    m, r, c = lax.axis_index("section"), lax.axis_index("row"), lax.axis_index("col")
    me = r * COLS + c
    other = 1 - m
    partner = (other, r, c)

    z, y = c // 4, lax.rem(c, 4)

    def step4(v):
        return jnp.where(v == 0, 2, jnp.where(v == 3, 0, 2 * v - 1))

    def column(k):
        return lax.rem(z + step4(k // 4), 4) * 4 + lax.rem(y + step4(lax.rem(k, 4)), 4)

    def each_peer(visit, with_own_place):
        def four(k, carry):
            to_c = column(k)
            for step in (2, 1, 3):
                visit(lax.rem(r + step, 4), to_c)
            if with_own_place:
                visit(r, to_c)
            else:
                pl.when(k < COLS - 1)(lambda: visit(r, to_c))
            return carry

        lax.fori_loop(0, COLS, four, 0)

    loads = [
        pltpu.make_async_copy(src, dst, isem.at[n])
        for n, (src, dst) in enumerate(
            [
                (act_ref.at[m], act_s.at[m]), (act_ref.at[other], act_s.at[other]), (cot_ref.at[m], cot_s),
                (proj_ref, w_s.at[m, :, pl.ds(0, 512)]), (gatew_ref, w_s.at[m, :, pl.ds(512, 128)]), (outw_ref, wo_s.at[m]),
                (lng_ref, vec_s.at[m, pl.ds(0, 1)]), (lnb_ref, vec_s.at[m, pl.ds(1, 1)]),
                (og_ref, vec_s.at[m, pl.ds(2, 1)]), (ob_ref, vec_s.at[m, pl.ds(3, 1)]),
                (mask_ref, mask_v), (mask_ref, mask_sm),
            ]
        )
    ]
    for load in loads:
        load.start()

    barrier = pltpu.get_barrier_semaphore()

    def greet(core):
        def visit(to_r, to_c):
            pl.semaphore_signal(barrier, inc=1, device_id=(core, to_r, to_c), device_id_type=MESH)

        return visit

    each_peer(greet(m), False)
    each_peer(greet(other), True)
    for load in loads[3:] + loads[:2]:
        load.wait()
    vec_s[m, 4:8] = jnp.zeros((4, 128), F32)

    low = lax.broadcasted_iota(jnp.int32, (128, 128), 1) < 64
    low1 = lax.broadcasted_iota(jnp.int32, (8, 128), 1) < 64

    def exchange(src, dst, phase, sec):
        def send(to_r, to_c):
            pltpu.make_async_remote_copy(
                src.at[sec, to_r * COLS + to_c], dst.at[sec, me], ssem.at[phase, sec], rsem.at[phase, sec],
                device_id=(m, to_r, to_c), device_id_type=MESH,
            ).start()

        each_peer(send, False)
        dst[sec, me] = src[sec, me]

    def exchange_lr():
        def send(dest):
            def visit(to_r, to_c):
                pltpu.make_async_remote_copy(
                    send_lr.at[dest, to_r * COLS + to_c], recv_lr.at[m, me], ssem.at[LR, dest], rsem.at[LR, m],
                    device_id=(dest, to_r, to_c), device_id_type=MESH,
                ).start()

            return visit

        each_peer(send(other), True)
        each_peer(send(m), False)
        recv_lr[m, me] = send_lr[m, me]

    def arrived_lr(sec):
        @pl.when(m == sec)
        def _():
            arrived(recv_lr, LR, sec)

        @pl.when(m != sec)
        def _():
            part = recv_lr.at[sec]
            pltpu.make_async_copy(part, part, rsem.at[LR, sec]).wait()


    def arrived(dst, phase, sec):
        part = dst.at[sec, pl.ds(0, PEERS - 1)]
        pltpu.make_async_copy(part, part, rsem.at[phase, sec]).wait()

    def sent(src, phase, sec):
        part = src.at[sec, pl.ds(0, PEERS - 1)]
        pltpu.make_async_copy(part, part, ssem.at[phase, sec]).wait()

    def lanes(b):
        return pl.ds(pl.multiple_of(b * WIDE, WIDE), WIDE)

    def cells_to_lanes(src, b):
        out = []
        for u in range(2):
            t = 2 * b + u
            rows = jnp.concatenate([src[pl.ds(t, 64, stride=16), :], src[pl.ds(t + 8, 64, stride=16), :]], axis=0)
            out.append(rows.T)
        return jnp.concatenate(out, axis=1)

    def lanes_to_cells(value, dst, b):
        for u in range(2):
            t = 2 * b + u
            rows = value[:, 128 * u:128 * u + 128].T
            dst[pl.ds(t, 64, stride=16), :] = rows[:64]
            dst[pl.ds(t + 8, 64, stride=16), :] = rows[64:]

    def spread(value, dst, b):
        for u in range(2):
            dst[pl.ds(2 * b + u, 128, stride=8), :] = value[:, 128 * u:128 * u + 128]

    def gathered(src, b):
        return jnp.concatenate([src[pl.ds(2 * b + u, 128, stride=8), :] for u in range(2)], axis=1)

    def wide(g):
        return jnp.concatenate([g, g], axis=1)

    is_even = lax.rem(r, 2) == 0
    for n in range(2):
        whole = mask_v[n:n + 1, :].astype(F32)
        half = jnp.broadcast_to(jnp.where(r >= 2, whole[:, 128:], whole[:, :128]), (8, 128))
        turned = pltpu.roll(half, 64, 1)
        mask_i = jnp.where(low1, jnp.where(is_even, half, turned), jnp.where(is_even, turned, half))
        for t in range(8):
            first = mask_sm[n, c * 16 + t].astype(F32)
            second = mask_sm[n, c * 16 + 8 + t].astype(F32)
            mask_s[n, :, 128 * t:128 * t + 128] = mask_i * jnp.where(low1, first, second)

    def prepare(sec):
        wt_s[sec] = w_s[sec].astype(F32).T.astype(BF16)
        wot_s[sec] = wo_s[sec].astype(F32).T.astype(BF16)
        for v in range(4):
            gain_s[sec, v] = jnp.broadcast_to(vec_s[sec, v:v + 1, :], (128, 128)).T

    def front(sec, source, save, target):
        xf[...] = source[...].astype(F32)

        def block(b, carry):
            at = lanes(b)
            x = cells_to_lanes(xf, b)
            centred = x - mean0(x)
            inv = lax.rsqrt(mean0(centred * centred) + EPSILON)
            hat = centred * inv
            nrm = (hat * wide(gain_s[sec, 0]) + wide(gain_s[sec, 1])).astype(BF16)
            lin_a = dot(wt_s[sec, 0:128], nrm)
            gate_a = sigmoid(dot(wt_s[sec, 128:256], nrm))
            lin_b = dot(wt_s[sec, 256:384], nrm)
            gate_b = sigmoid(dot(wt_s[sec, 384:512], nrm))
            if target is not None:
                mask = mask_s[target, 0:1, at]
                spread(gate_a * lin_a * mask, scr_a, b)
                spread(gate_b * lin_b * mask, scr_b, b)
            if save:
                hat_s[sec, :, at] = hat
                inv_s[sec, :, at] = jnp.broadcast_to(inv, (8, WIDE))
                nrm_s[sec, :, at] = nrm
                la_s[sec, :, at] = lin_a
                ga_s[sec, :, at] = gate_a
                lb_s[sec, :, at] = lin_b
                gb_s[sec, :, at] = gate_b
                go_s[sec, :, at] = sigmoid(dot(wt_s[sec, 512:640], nrm))
            return carry

        lax.fori_loop(0, 4, block, 0)
        if target is not None:
            send_lr[target, :, 0:16, :] = scr_a[...].reshape(PEERS, 16, 128).astype(BF16)
            send_lr[target, :, 16:32, :] = scr_b[...].reshape(PEERS, 16, 128).astype(BF16)

    def assemble(src, sec, at, dst, first):
        for q in range(2):
            even = src[sec, 32 * q:32 * q + 16, at:at + 16, :].astype(F32)
            odd = src[sec, 32 * q + 16:32 * q + 32, at:at + 16, :].astype(F32)
            for ch in range(2):
                a = even[:, 8 * ch:8 * ch + 8, :].reshape(128, 128)
                b = odd[:, 8 * ch:8 * ch + 8, :].reshape(128, 128)
                k0 = jnp.where(low, a, pltpu.roll(b, 64, 1)).reshape(16, 1, 8, 128)
                k1 = jnp.where(low, pltpu.roll(a, 64, 1), b).reshape(16, 1, 8, 128)
                full = jnp.concatenate([k0, k1], axis=1).reshape(256, 128)
                dst[first + ch, :, 128 * q:128 * q + 128] = full.astype(BF16)

    def take_apart(pair, dst, sec, at):
        for q in range(2):
            evens, odds = [], []
            for y in pair:
                y4 = y[:, 128 * q:128 * q + 128].reshape(16, 2, 8, 128)
                y0 = y4[:, 0].reshape(128, 128)
                y1 = y4[:, 1].reshape(128, 128)
                evens.append(jnp.where(low, y0, pltpu.roll(y1, 64, 1)).reshape(16, 8, 128))
                odds.append(jnp.where(low, pltpu.roll(y0, 64, 1), y1).reshape(16, 8, 128))
            dst[sec, 32 * q:32 * q + 16, at:at + 16, :] = jnp.concatenate(evens, axis=1).astype(BF16)
            dst[sec, 32 * q + 16:32 * q + 32, at:at + 16, :] = jnp.concatenate(odds, axis=1).astype(BF16)

    def mix(sec):
        arrived_lr(sec)
        assemble(recv_lr, sec, 0, lt_s, 2 * sec)
        assemble(recv_lr, sec, 16, rt_s, 2 * sec)
        pair = [dot(rt_s[2 * sec + ch], lt_s[2 * sec + ch], 0, 0) for ch in range(2)]
        take_apart(pair, send_m, sec, 0)
        exchange(send_m, recv_m, MIX, sec)

    def out_forward(sec):
        arrived(recv_m, MIX, sec)
        scr_a[...] = recv_m[sec].astype(F32).reshape(N, 128)

        def block(b, carry):
            at = lanes(b)
            x = gathered(scr_a, b)
            centred = x - mean0(x)
            inv = lax.rsqrt(mean0(centred * centred) + EPSILON)
            hat = centred * inv
            mn = (hat * wide(gain_s[sec, 2]) + wide(gain_s[sec, 3])).astype(BF16)
            mhat_s[sec, :, at] = hat
            minv_s[sec, :, at] = jnp.broadcast_to(inv, (8, WIDE))
            mn_s[sec, :, at] = mn
            gate = go_s[sec, :, at]
            oc_s[sec, :, at] = dot(wot_s[sec], mn) * gate * (1.0 - gate)
            return carry

        lax.fori_loop(0, 4, block, 0)

    def out_backward(sec):
        acc_s[sec, 2] = jnp.zeros((128, WIDE), F32)
        acc_s[sec, 3] = jnp.zeros((128, WIDE), F32)

        def block(b, carry):
            at = lanes(b)
            up = up_s[sec, :, at]
            dout = (up * go_s[sec, :, at]).astype(BF16)
            dout_s[sec, :, at] = dout
            dpre_s[sec, 512:640, at] = (up * oc_s[sec, :, at]).astype(BF16)
            dn = dot(wo_s[sec], dout)
            hat = mhat_s[sec, :, at]
            acc_s[sec, 2] += dn * hat
            acc_s[sec, 3] += dn
            e = dn * wide(gain_s[sec, 2])
            d = (e - mean0(e) - hat * mean0(e * hat)) * minv_s[sec, 0:1, at]
            spread(d, scr_b, b)
            return carry

        lax.fori_loop(0, 4, block, 0)
        send_d[sec] = scr_b[...].reshape(PEERS, 16, 128).astype(BF16)
        exchange(send_d, recv_d, DMIX, sec)

    def out_before(sec):
        def block(b, carry):
            at = lanes(b)
            dout = (up_s[sec, :, at] * go_s[sec, :, at]).astype(BF16)
            dout_s[sec, :, at] = dout
            dn_s[:, at] = dot(wo_s[sec], dout)
            return carry

        lax.fori_loop(0, 4, block, 0)

    def out_chain(sec):
        arrived(recv_m, MIX, sec)
        scr_a[...] = recv_m[sec].astype(F32).reshape(N, 128)

        def block(b, carry):
            at = lanes(b)
            x = gathered(scr_a, b)
            centred = x - mean0(x)
            inv = lax.rsqrt(mean0(centred * centred) + EPSILON)
            hat = centred * inv
            mhat_s[sec, :, at] = hat
            e = dn_s[:, at] * wide(gain_s[sec, 2])
            spread((e - mean0(e) - hat * mean0(e * hat)) * inv, scr_b, b)
            return carry

        lax.fori_loop(0, 4, block, 0)
        send_d[sec] = scr_b[...].reshape(PEERS, 16, 128).astype(BF16)
        exchange(send_d, recv_d, DMIX, sec)

    def out_after(sec):
        acc_s[sec, 2] = jnp.zeros((128, WIDE), F32)
        acc_s[sec, 3] = jnp.zeros((128, WIDE), F32)

        def block(b, carry):
            at = lanes(b)
            hat = mhat_s[sec, :, at]
            mn = (hat * wide(gain_s[sec, 2]) + wide(gain_s[sec, 3])).astype(BF16)
            mn_s[sec, :, at] = mn
            gate = go_s[sec, :, at]
            dgate = up_s[sec, :, at] * dot(wot_s[sec], mn) * gate * (1.0 - gate)
            dpre_s[sec, 512:640, at] = dgate.astype(BF16)
            dn = dn_s[:, at]
            acc_s[sec, 2] += dn * hat
            acc_s[sec, 3] += dn
            return carry

        lax.fori_loop(0, 4, block, 0)

    def products_back(sec):
        arrived(recv_d, DMIX, sec)
        assemble(recv_d, sec, 0, dt_s, 0)
        pair = [dot(rt_s[2 * sec + ch], dt_s[ch]) for ch in range(2)]
        take_apart(pair, send_g, sec, 0)
        pair = [dot(lt_s[2 * sec + ch], dt_s[ch], 1, 1) for ch in range(2)]
        take_apart(pair, send_g, sec, 16)
        exchange(send_g, recv_g, DLR, sec)

    def in_part(sec):
        acc_s[sec, 0] = jnp.zeros((128, WIDE), F32)
        acc_s[sec, 1] = jnp.zeros((128, WIDE), F32)
        arrived(recv_g, DLR, sec)
        scr_a[...] = recv_g[sec, :, 0:16, :].astype(F32).reshape(N, 128)
        scr_b[...] = recv_g[sec, :, 16:32, :].astype(F32).reshape(N, 128)

        def block(b, carry):
            at = lanes(b)
            mask = mask_s[m, 0:1, at]
            gate = ga_s[sec, :, at]
            dg = gathered(scr_a, b) * gate * mask
            dpre_s[sec, 0:128, at] = dg.astype(BF16)
            dpre_s[sec, 128:256, at] = (dg * la_s[sec, :, at] * (1.0 - gate)).astype(BF16)
            gate = gb_s[sec, :, at]
            dg = gathered(scr_b, b) * gate * mask
            dpre_s[sec, 256:384, at] = dg.astype(BF16)
            dpre_s[sec, 384:512, at] = (dg * lb_s[sec, :, at] * (1.0 - gate)).astype(BF16)
            din = dot(w_s[sec], dpre_s[sec, :, at])
            hat = hat_s[sec, :, at]
            acc_s[sec, 0] += din * hat
            acc_s[sec, 1] += din
            f = din * wide(gain_s[sec, 0])
            up = up_s[sec, :, at] + (f - mean0(f) - hat * mean0(f * hat)) * inv_s[sec, 0:1, at]
            up_s[sec - 1 if sec > 0 else 2, :, at] = up
            return carry

        lax.fori_loop(0, 4, block, 0)

    def back_to_cells(sec):
        def block(b, carry):
            lanes_to_cells(up_s[sec - 1 if sec > 0 else 2, :, lanes(b)], pgb.at[sec], b)
            return carry

        lax.fori_loop(0, 4, block, 0)

    def early_grads(sec):
        g = dot(nrm_s[sec], dpre_s[sec, 512:640, :], 1, 1)
        gs[sec, 32:40] = g.reshape(8, 16, 128).astype(BF16)
        g = dot(mn_s[sec], dout_s[sec], 1, 1)
        gs[sec, 40:48] = g.reshape(8, 16, 128).astype(BF16)
        scatter_grads(sec, True)

    def late_grads(sec):
        for o in range(4):
            g = dot(nrm_s[sec], dpre_s[sec, 128 * o:128 * o + 128, :], 1, 1)
            gs[sec, 8 * o:8 * o + 8] = g.reshape(8, 16, 128).astype(BF16)
        rows = []
        for v in range(4):
            total = (acc_s[sec, v, :, 0:128] + acc_s[sec, v, :, 128:256]).T
            rows.append(jnp.sum(total, axis=0, keepdims=True))
        rows = jnp.concatenate(rows + [jnp.zeros((4, 128), F32)], axis=0)
        high = rows.astype(BF16).astype(F32)
        gs[sec, 48] = jnp.concatenate([high, rows - high], axis=0).astype(BF16)
        scatter_grads(sec, False)

    def scatter_grads(sec, early):
        def give(to_r, to_c):
            d = to_r * COLS + to_c
            mine = jnp.logical_and(m == sec, d == me)

            @pl.when(jnp.logical_not(mine))
            def _():
                pltpu.make_async_remote_copy(
                    gs.at[sec, d], recv_b.at[m * PEERS + me], ssem.at[RS, sec], rsem.at[RS, 0],
                    device_id=(sec, to_r, to_c), device_id_type=MESH,
                ).start()

            @pl.when(mine)
            def _():
                recv_b[m * PEERS + me] = gs[sec, d]

        def send(k, carry):
            to_c = column(k)
            if early:
                give(2, to_c)
            else:
                give(0, to_c)
                give(1, to_c)
            return carry

        lax.fori_loop(0, COLS, send, 0)
        if not early:
            give(3, 0)

    def gather_grads():
        @pl.when(me < OWNERS)
        def _():
            part = recv_b.at[pl.ds(0, 2 * PEERS - 1)]
            pltpu.make_async_copy(part, part, rsem.at[RS, 0]).wait()
            recv_o[me] = jnp.sum(recv_b[...].astype(F32), axis=0)

            def give(to_r, to_c):
                pltpu.make_async_remote_copy(
                    recv_o.at[me], recv_o.at[me], dsem.at[0], dsem.at[1],
                    device_id=(m, to_r, to_c), device_id_type=MESH,
                ).start()

            each_peer(give, False)

    prepare(m)
    front(m, act_s.at[m], True, m)
    front(m, act_s.at[other], False, other)
    pl.semaphore_wait(barrier, 2 * PEERS - 1)

    @pl.when(m == 1)
    def _():
        exchange_lr()

    swaps = [
        pltpu.make_async_remote_copy(
            src, dst, psend.at[n], precv.at[n], device_id=partner, device_id_type=MESH
        )
        for n, (src, dst) in enumerate(
            [(act_s.at[other], xs.at[m]), (w_s.at[m], w_s.at[m]), (wo_s.at[m], wo_s.at[m]), (vec_s.at[m], vec_s.at[m])]
        )
    ]
    for swap in swaps:
        swap.start()

    def turn(b, carry):
        up_s[1, :, lanes(b)] = cells_to_lanes(cot_s, b)
        return carry

    loads[2].wait()
    lax.fori_loop(0, 4, turn, 0)
    for swap in swaps:
        swap.wait_recv()
    prepare(other)
    front(other, xs.at[other], True, None)
    out_before(1)

    mix(1)

    @pl.when(m == 0)
    def _():
        exchange_lr()

    out_chain(1)
    mix(0)
    out_after(1)
    early_grads(1)
    products_back(1)
    out_forward(0)
    in_part(1)
    out_backward(0)
    late_grads(1)
    back_to_cells(1)
    handed = pltpu.make_async_remote_copy(
        pgb.at[other], pg_ref.at[m], psend.at[PG_COPY], precv.at[PG_COPY], device_id=partner, device_id_type=MESH
    )

    @pl.when(m == 0)
    def _():
        handed.start()

    @pl.when(m == 1)
    def _():
        pg_ref[1] = pgb[1]

    products_back(0)
    early_grads(0)

    in_part(0)
    late_grads(0)
    back_to_cells(0)

    @pl.when(m == 1)
    def _():
        handed.start()

    @pl.when(m == 0)
    def _():
        pg_ref[0] = pgb[0]

    gather_grads()

    for src, phase in ((send_m, MIX), (send_d, DMIX), (send_g, DLR)):
        for sec in range(2):
            sent(src, phase, sec)
    sent(send_lr, LR, m)
    part = send_lr.at[other]
    pltpu.make_async_copy(part, part, ssem.at[LR, other]).wait()
    for sec in range(2):
        own_rows = jnp.logical_and(m == sec, me < OWNERS)
        for count, which in ((OWNERS - 1, own_rows), (OWNERS, jnp.logical_not(own_rows))):

            @pl.when(which)
            def _(count=count, sec=sec):
                part = gs.at[sec, pl.ds(0, count)]
                pltpu.make_async_copy(part, part, ssem.at[RS, sec]).wait()

    for swap in swaps:
        swap.wait_send()
    handed.wait()

    @pl.when(me >= OWNERS)
    def _():
        part = recv_o.at[pl.ds(0, OWNERS)]
        pltpu.make_async_copy(part, part, dsem.at[1]).wait()

    @pl.when(me < OWNERS)
    def _():
        part = recv_o.at[pl.ds(0, OWNERS - 1)]
        pltpu.make_async_copy(part, part, dsem.at[1]).wait()
        part = recv_o.at[pl.ds(0, PEERS - 1)]
        pltpu.make_async_copy(part, part, dsem.at[0]).wait()


def write_out(pg_in, o_in, pg_ref, glng_ref, glnb_ref, gproj_ref, ggate_ref, gog_ref, gob_ref, gow_ref, held, o_ref, sem_in, sem_out, sem_o):
    rows = pltpu.make_async_copy(o_in.at[pl.ds(0, OWNERS)], o_ref, sem_o.at[0])
    parts = [pl.ds(n * 256, 256) for n in range(8)]
    come = [pltpu.make_async_copy(pg_in.at[p], held.at[p], sem_in.at[n]) for n, p in enumerate(parts)]
    go = [pltpu.make_async_copy(held.at[p], pg_ref.at[p], sem_out.at[n]) for n, p in enumerate(parts)]
    for copy in come:
        copy.start()
    rows.start()
    for copy_in, copy_out in zip(come, go):
        copy_in.wait()
        copy_out.start()
    rows.wait()
    for o in range(4):
        gproj_ref[:, 128 * o:128 * o + 128] = o_ref[8 * o:8 * o + 8].reshape(128, 128)
    ggate_ref[...] = o_ref[32:40].reshape(128, 128)
    gow_ref[...] = o_ref[40:48].reshape(128, 128)
    for v, ref in enumerate((glng_ref, glnb_ref, gog_ref, gob_ref)):
        ref[...] = o_ref[48, v:v + 1, :] + o_ref[48, 8 + v:9 + v, :]
    for copy in go:
        copy.wait()


def on_device(act, cot, mask, lng, lnb, proj, gatew, og, ob, outw):
    vmem = pl.BlockSpec(memory_space=pltpu.VMEM)
    anywhere = pl.BlockSpec(memory_space=pl.ANY)

    def v(shape, dtype=F32):
        return pltpu.VMEM(shape, dtype)

    sds = jax.ShapeDtypeStruct
    pg, rows = pl.pallas_call(
        kernel,
        out_shape=(sds((2, N, 128), F32), sds((PEERS, 16, 128), F32)),
        in_specs=[anywhere] * 10,
        out_specs=(vmem,) * 2,
        scratch_shapes=[
            v((2, N, 128), BF16), v((N, 128)), v((2, 256), jnp.int32), pltpu.SMEM((2, 256), jnp.int32),
            v((2, N, 128), BF16), v((2, 128, 640), BF16), v((2, 128, 128), BF16), v((2, 8, 128)), v((N, 128)),
            v((2, 640, 128), BF16), v((2, 128, 128), BF16), v((2, 4, 128, 128)), v((2, 8, N)),
            v((2, 128, N)), v((2, 8, N)), v((2, 128, N), BF16),
            v((2, 128, N)), v((2, 128, N)), v((2, 128, N)), v((2, 128, N)), v((2, 128, N)),
            v((2, 128, N)), v((2, 8, N)), v((2, 128, N), BF16), v((2, 128, N)), v((3, 128, N)),
            v((2, 128, N), BF16), v((2, 640, N), BF16), v((2, 4, 128, WIDE)),
            v((128, N)), v((N, 128)), v((N, 128)), v((4, 256, 256), BF16), v((4, 256, 256), BF16), v((2, 256, 256), BF16),
            v((2, PEERS, 32, 128), BF16), v((2, PEERS, 32, 128), BF16),
            v((2, PEERS, 16, 128), BF16), v((2, PEERS, 16, 128), BF16),
            v((2, PEERS, 16, 128), BF16), v((2, PEERS, 16, 128), BF16),
            v((2, PEERS, 32, 128), BF16), v((2, PEERS, 32, 128), BF16),
            v((2, N, 128)), v((2, OWNERS, 16, 128), BF16), v((2 * PEERS, 16, 128), BF16),
            pltpu.SemaphoreType.DMA((12,)), pltpu.SemaphoreType.DMA((5,)), pltpu.SemaphoreType.DMA((5,)),
            pltpu.SemaphoreType.DMA((5, 2)), pltpu.SemaphoreType.DMA((5, 2)),
            pltpu.SemaphoreType.DMA((2,)),
        ],
        compiler_params=pltpu.CompilerParams(
            collective_id=1, has_side_effects=True, vmem_limit_bytes=56 * 2**20
        ),
    )(
        act.reshape(2, N, 128), cot.reshape(2, N, 128), mask, lng, lnb, proj[0], gatew[0], og, ob, outw[0]
    )
    pg, glng, glnb, gproj, ggate, gog, gob, gow = pl.pallas_call(
        write_out,
        out_shape=(
            sds((2 * N, 128), F32), sds((1, 128), F32), sds((1, 128), F32), sds((128, 512), F32),
            sds((128, 128), F32), sds((1, 128), F32), sds((1, 128), F32), sds((128, 128), F32),
        ),
        in_specs=[anywhere, anywhere],
        out_specs=(anywhere,) + (vmem,) * 7,
        scratch_shapes=[
            v((2 * N, 128)), v((OWNERS, 16, 128)),
            pltpu.SemaphoreType.DMA((8,)), pltpu.SemaphoreType.DMA((8,)), pltpu.SemaphoreType.DMA((1,)),
        ],
    )(pg.reshape(2 * N, 128), rows)
    return (
        pg.reshape(1, 2, 64, 16, 128), glng, glnb, gproj[None], ggate[None], gog, gob, gow[None],
    )


def solution(mesh):
    vector, matrix = P("section", None), P("section", None, None)
    grid = P("section", None, "row", "col", None)
    return jax.shard_map(
        on_device,
        mesh=mesh,
        in_specs=(grid, P(None, "row", "col", None), P(), vector, vector, matrix, matrix, vector, vector, matrix),
        out_specs=(grid, vector, vector, matrix, matrix, vector, vector, matrix),
        check_vma=False,
    )
```

```python
import jax
import jax.numpy as jnp
from jax import lax
from jax.experimental import pallas as pl
from jax.experimental.pallas import tpu as pltpu
from jax.sharding import PartitionSpec as P

EPSILON = 1e-05
MESH = pl.DeviceIdType.MESH
F32 = jnp.float32
BF16 = jnp.bfloat16
ROWS = 4
COLS = 16
PEERS = ROWS * COLS
N = 1024
WIDE = 256

X_COPY, W_COPY, O_COPY, V_COPY, PG_COPY = range(5)
LR, MIX, DMIX, DLR, RS = range(5)
OWNERS = 49


def sigmoid(v):
    return 0.5 * jnp.tanh(0.5 * v) + 0.5


def mean0(v):
    return jnp.mean(v, axis=0, keepdims=True)


def dot(a, b, ca=1, cb=0):
    return lax.dot_general(a, b, (((ca,), (cb,)), ((), ())), preferred_element_type=F32)


def kernel(
    act_ref, cot_ref, mask_ref, lng_ref, lnb_ref, proj_ref, gatew_ref, og_ref, ob_ref, outw_ref,
    pg_ref, recv_o,
    act_s, cot_s, mask_v, mask_sm, xs, w_s, wo_s, vec_s, xf, wt_s, wot_s, gain_s, mask_s,
    hat_s, inv_s, nrm_s, la_s, ga_s, lb_s, gb_s, go_s,
    mhat_s, minv_s, mn_s, oc_s, up_s, dout_s, dpre_s, acc_s,
    dn_s, scr_a, scr_b, lt_s, rt_s, dt_s,
    send_lr, recv_lr, send_m, recv_m, send_d, recv_d, send_g, recv_g,
    pgb, gs, recv_b,
    isem, psend, precv, ssem, rsem, dsem,
):
    m, r, c = lax.axis_index("section"), lax.axis_index("row"), lax.axis_index("col")
    me = r * COLS + c
    other = 1 - m
    partner = (other, r, c)

    z, y = c // 4, lax.rem(c, 4)

    def step4(v):
        return jnp.where(v == 0, 2, jnp.where(v == 3, 0, 2 * v - 1))

    def column(k):
        return lax.rem(z + step4(k // 4), 4) * 4 + lax.rem(y + step4(lax.rem(k, 4)), 4)

    def each_peer(visit, with_own_place):
        def four(k, carry):
            to_c = column(k)
            for step in (2, 1, 3):
                visit(lax.rem(r + step, 4), to_c)
            if with_own_place:
                visit(r, to_c)
            else:
                pl.when(k < COLS - 1)(lambda: visit(r, to_c))
            return carry

        lax.fori_loop(0, COLS, four, 0)

    loads = [
        pltpu.make_async_copy(src, dst, isem.at[n])
        for n, (src, dst) in enumerate(
            [
                (act_ref.at[m], act_s.at[m]), (act_ref.at[other], act_s.at[other]), (cot_ref.at[m], cot_s),
                (proj_ref, w_s.at[m, :, pl.ds(0, 512)]), (gatew_ref, w_s.at[m, :, pl.ds(512, 128)]), (outw_ref, wo_s.at[m]),
                (lng_ref, vec_s.at[m, pl.ds(0, 1)]), (lnb_ref, vec_s.at[m, pl.ds(1, 1)]),
                (og_ref, vec_s.at[m, pl.ds(2, 1)]), (ob_ref, vec_s.at[m, pl.ds(3, 1)]),
                (mask_ref, mask_v), (mask_ref, mask_sm),
            ]
        )
    ]
    barrier = pltpu.get_barrier_semaphore()

    def greet(core):
        def visit(to_r, to_c):
            pl.semaphore_signal(barrier, inc=1, device_id=(core, to_r, to_c), device_id_type=MESH)

        return visit

    @pl.when(m == 0)
    def _():
        each_peer(greet(other), True)
        each_peer(greet(m), False)

    @pl.when(m == 1)
    def _():
        each_peer(greet(m), False)
        each_peer(greet(other), True)

    for load in loads:
        load.start()

    for load in loads[3:]:
        load.wait()
    vec_s[m, 4:8] = jnp.zeros((4, 128), F32)

    low = lax.broadcasted_iota(jnp.int32, (128, 128), 1) < 64
    low1 = lax.broadcasted_iota(jnp.int32, (8, 128), 1) < 64

    def exchange(src, dst, phase, sec):
        def send(to_r, to_c):
            pltpu.make_async_remote_copy(
                src.at[sec, to_r * COLS + to_c], dst.at[sec, me], ssem.at[phase, sec], rsem.at[phase, sec],
                device_id=(m, to_r, to_c), device_id_type=MESH,
            ).start()

        each_peer(send, False)
        dst[sec, me] = src[sec, me]

    def exchange_lr(to_other=True, to_own=True):
        def send(dest):
            def visit(to_r, to_c):
                pltpu.make_async_remote_copy(
                    send_lr.at[dest, to_r * COLS + to_c], recv_lr.at[m, me], ssem.at[LR, dest], rsem.at[LR, m],
                    device_id=(dest, to_r, to_c), device_id_type=MESH,
                ).start()

            return visit

        if to_other:
            each_peer(send(other), True)
        if to_own:
            each_peer(send(m), False)
            recv_lr[m, me] = send_lr[m, me]

    def arrived_lr(sec):
        @pl.when(m == sec)
        def _():
            arrived(recv_lr, LR, sec)

        @pl.when(m != sec)
        def _():
            part = recv_lr.at[sec]
            pltpu.make_async_copy(part, part, rsem.at[LR, sec]).wait()


    def arrived(dst, phase, sec):
        part = dst.at[sec, pl.ds(0, PEERS - 1)]
        pltpu.make_async_copy(part, part, rsem.at[phase, sec]).wait()

    def sent(src, phase, sec):
        part = src.at[sec, pl.ds(0, PEERS - 1)]
        pltpu.make_async_copy(part, part, ssem.at[phase, sec]).wait()

    def lanes(b):
        return pl.ds(pl.multiple_of(b * WIDE, WIDE), WIDE)

    def cells_to_lanes(src, b):
        out = []
        for u in range(2):
            t = 2 * b + u
            rows = jnp.concatenate([src[pl.ds(t, 64, stride=16), :], src[pl.ds(t + 8, 64, stride=16), :]], axis=0)
            out.append(rows.T)
        return jnp.concatenate(out, axis=1)

    def lanes_to_cells(value, dst, b):
        for u in range(2):
            t = 2 * b + u
            rows = value[:, 128 * u:128 * u + 128].T
            dst[pl.ds(t, 64, stride=16), :] = rows[:64]
            dst[pl.ds(t + 8, 64, stride=16), :] = rows[64:]

    def spread(value, dst, b):
        for u in range(2):
            dst[pl.ds(2 * b + u, 128, stride=8), :] = value[:, 128 * u:128 * u + 128]

    def gathered(src, b):
        return jnp.concatenate([src[pl.ds(2 * b + u, 128, stride=8), :] for u in range(2)], axis=1)

    def wide(g):
        return jnp.concatenate([g, g], axis=1)

    is_even = lax.rem(r, 2) == 0
    for n in range(2):
        whole = mask_v[n:n + 1, :].astype(F32)
        half = jnp.broadcast_to(jnp.where(r >= 2, whole[:, 128:], whole[:, :128]), (8, 128))
        turned = pltpu.roll(half, 64, 1)
        mask_i = jnp.where(low1, jnp.where(is_even, half, turned), jnp.where(is_even, turned, half))
        for t in range(8):
            first = mask_sm[n, c * 16 + t].astype(F32)
            second = mask_sm[n, c * 16 + 8 + t].astype(F32)
            mask_s[n, :, 128 * t:128 * t + 128] = mask_i * jnp.where(low1, first, second)

    def prepare(sec):
        wt_s[sec] = w_s[sec].astype(F32).T.astype(BF16)
        wot_s[sec] = wo_s[sec].astype(F32).T.astype(BF16)
        for v in range(4):
            gain_s[sec, v] = jnp.broadcast_to(vec_s[sec, v:v + 1, :], (128, 128)).T

    def front(sec, source, save, target):
        xf[...] = source[...].astype(F32)

        def block(b, carry):
            at = lanes(b)
            x = cells_to_lanes(xf, b)
            centred = x - mean0(x)
            inv = lax.rsqrt(mean0(centred * centred) + EPSILON)
            hat = centred * inv
            nrm = (hat * wide(gain_s[sec, 0]) + wide(gain_s[sec, 1])).astype(BF16)
            lin_a = dot(wt_s[sec, 0:128], nrm)
            gate_a = sigmoid(dot(wt_s[sec, 128:256], nrm))
            lin_b = dot(wt_s[sec, 256:384], nrm)
            gate_b = sigmoid(dot(wt_s[sec, 384:512], nrm))
            if target is not None:
                mask = mask_s[target, 0:1, at]
                spread(gate_a * lin_a * mask, scr_a, b)
                spread(gate_b * lin_b * mask, scr_b, b)
            if save:
                hat_s[sec, :, at] = hat
                inv_s[sec, :, at] = jnp.broadcast_to(inv, (8, WIDE))
                nrm_s[sec, :, at] = nrm
                la_s[sec, :, at] = lin_a
                ga_s[sec, :, at] = gate_a
                lb_s[sec, :, at] = lin_b
                gb_s[sec, :, at] = gate_b
                go_s[sec, :, at] = sigmoid(dot(wt_s[sec, 512:640], nrm))
            return carry

        lax.fori_loop(0, 4, block, 0)
        if target is not None:
            send_lr[target, :, 0:16, :] = scr_a[...].reshape(PEERS, 16, 128).astype(BF16)
            send_lr[target, :, 16:32, :] = scr_b[...].reshape(PEERS, 16, 128).astype(BF16)

    def assemble(src, sec, at, dst, first):
        for q in range(2):
            even = src[sec, 32 * q:32 * q + 16, at:at + 16, :].astype(F32)
            odd = src[sec, 32 * q + 16:32 * q + 32, at:at + 16, :].astype(F32)
            for ch in range(2):
                a = even[:, 8 * ch:8 * ch + 8, :].reshape(128, 128)
                b = odd[:, 8 * ch:8 * ch + 8, :].reshape(128, 128)
                k0 = jnp.where(low, a, pltpu.roll(b, 64, 1)).reshape(16, 1, 8, 128)
                k1 = jnp.where(low, pltpu.roll(a, 64, 1), b).reshape(16, 1, 8, 128)
                full = jnp.concatenate([k0, k1], axis=1).reshape(256, 128)
                dst[first + ch, :, 128 * q:128 * q + 128] = full.astype(BF16)

    def take_apart(pair, dst, sec, at):
        for q in range(2):
            evens, odds = [], []
            for y in pair:
                y4 = y[:, 128 * q:128 * q + 128].reshape(16, 2, 8, 128)
                y0 = y4[:, 0].reshape(128, 128)
                y1 = y4[:, 1].reshape(128, 128)
                evens.append(jnp.where(low, y0, pltpu.roll(y1, 64, 1)).reshape(16, 8, 128))
                odds.append(jnp.where(low, pltpu.roll(y0, 64, 1), y1).reshape(16, 8, 128))
            dst[sec, 32 * q:32 * q + 16, at:at + 16, :] = jnp.concatenate(evens, axis=1).astype(BF16)
            dst[sec, 32 * q + 16:32 * q + 32, at:at + 16, :] = jnp.concatenate(odds, axis=1).astype(BF16)

    def mix(sec):
        arrived_lr(sec)
        assemble(recv_lr, sec, 0, lt_s, 2 * sec)
        assemble(recv_lr, sec, 16, rt_s, 2 * sec)
        pair = [dot(rt_s[2 * sec + ch], lt_s[2 * sec + ch], 0, 0) for ch in range(2)]
        take_apart(pair, send_m, sec, 0)
        exchange(send_m, recv_m, MIX, sec)

    def out_forward(sec):
        arrived(recv_m, MIX, sec)
        scr_a[...] = recv_m[sec].astype(F32).reshape(N, 128)

        def block(b, carry):
            at = lanes(b)
            x = gathered(scr_a, b)
            centred = x - mean0(x)
            inv = lax.rsqrt(mean0(centred * centred) + EPSILON)
            hat = centred * inv
            mn = (hat * wide(gain_s[sec, 2]) + wide(gain_s[sec, 3])).astype(BF16)
            mhat_s[sec, :, at] = hat
            minv_s[sec, :, at] = jnp.broadcast_to(inv, (8, WIDE))
            mn_s[sec, :, at] = mn
            gate = go_s[sec, :, at]
            oc_s[sec, :, at] = dot(wot_s[sec], mn) * gate * (1.0 - gate)
            return carry

        lax.fori_loop(0, 4, block, 0)

    def out_backward(sec):
        def block(b, carry):
            at = lanes(b)
            dout = (up_s[sec, :, at] * go_s[sec, :, at]).astype(BF16)
            dout_s[sec, :, at] = dout
            dn = dot(wo_s[sec], dout)
            dn_s[:, at] = dn
            hat = mhat_s[sec, :, at]
            e = dn * wide(gain_s[sec, 2])
            spread((e - mean0(e) - hat * mean0(e * hat)) * minv_s[sec, 0:1, at], scr_b, b)
            return carry

        lax.fori_loop(0, 4, block, 0)
        send_d[sec] = scr_b[...].reshape(PEERS, 16, 128).astype(BF16)
        exchange(send_d, recv_d, DMIX, sec)
        acc_s[sec, 2] = jnp.zeros((128, WIDE), F32)
        acc_s[sec, 3] = jnp.zeros((128, WIDE), F32)

        def rest(b, carry):
            at = lanes(b)
            dpre_s[sec, 512:640, at] = (up_s[sec, :, at] * oc_s[sec, :, at]).astype(BF16)
            dn = dn_s[:, at]
            acc_s[sec, 2] += dn * mhat_s[sec, :, at]
            acc_s[sec, 3] += dn
            return carry

        lax.fori_loop(0, 4, rest, 0)

    def out_before(sec):
        def block(b, carry):
            at = lanes(b)
            dout = (up_s[sec, :, at] * go_s[sec, :, at]).astype(BF16)
            dout_s[sec, :, at] = dout
            dn_s[:, at] = dot(wo_s[sec], dout)
            return carry

        lax.fori_loop(0, 4, block, 0)

    def out_chain(sec):
        arrived(recv_m, MIX, sec)
        scr_a[...] = recv_m[sec].astype(F32).reshape(N, 128)

        def block(b, carry):
            at = lanes(b)
            x = gathered(scr_a, b)
            centred = x - mean0(x)
            inv = lax.rsqrt(mean0(centred * centred) + EPSILON)
            hat = centred * inv
            mhat_s[sec, :, at] = hat
            e = dn_s[:, at] * wide(gain_s[sec, 2])
            spread((e - mean0(e) - hat * mean0(e * hat)) * inv, scr_b, b)
            return carry

        lax.fori_loop(0, 4, block, 0)
        send_d[sec] = scr_b[...].reshape(PEERS, 16, 128).astype(BF16)
        exchange(send_d, recv_d, DMIX, sec)

    def out_after(sec):
        acc_s[sec, 2] = jnp.zeros((128, WIDE), F32)
        acc_s[sec, 3] = jnp.zeros((128, WIDE), F32)

        def block(b, carry):
            at = lanes(b)
            hat = mhat_s[sec, :, at]
            mn = (hat * wide(gain_s[sec, 2]) + wide(gain_s[sec, 3])).astype(BF16)
            mn_s[sec, :, at] = mn
            gate = go_s[sec, :, at]
            dgate = up_s[sec, :, at] * dot(wot_s[sec], mn) * gate * (1.0 - gate)
            dpre_s[sec, 512:640, at] = dgate.astype(BF16)
            dn = dn_s[:, at]
            acc_s[sec, 2] += dn * hat
            acc_s[sec, 3] += dn
            return carry

        lax.fori_loop(0, 4, block, 0)

    def products_back(sec):
        arrived(recv_d, DMIX, sec)
        assemble(recv_d, sec, 0, dt_s, 0)
        pair = [dot(rt_s[2 * sec + ch], dt_s[ch]) for ch in range(2)]
        take_apart(pair, send_g, sec, 0)
        pair = [dot(lt_s[2 * sec + ch], dt_s[ch], 1, 1) for ch in range(2)]
        take_apart(pair, send_g, sec, 16)
        exchange(send_g, recv_g, DLR, sec)

    def in_part(sec):
        acc_s[sec, 0] = jnp.zeros((128, WIDE), F32)
        acc_s[sec, 1] = jnp.zeros((128, WIDE), F32)
        arrived(recv_g, DLR, sec)
        scr_a[...] = recv_g[sec, :, 0:16, :].astype(F32).reshape(N, 128)
        scr_b[...] = recv_g[sec, :, 16:32, :].astype(F32).reshape(N, 128)

        def block(b, carry):
            at = lanes(b)
            mask = mask_s[m, 0:1, at]
            gate = ga_s[sec, :, at]
            dg = gathered(scr_a, b) * gate * mask
            dpre_s[sec, 0:128, at] = dg.astype(BF16)
            dpre_s[sec, 128:256, at] = (dg * la_s[sec, :, at] * (1.0 - gate)).astype(BF16)
            gate = gb_s[sec, :, at]
            dg = gathered(scr_b, b) * gate * mask
            dpre_s[sec, 256:384, at] = dg.astype(BF16)
            dpre_s[sec, 384:512, at] = (dg * lb_s[sec, :, at] * (1.0 - gate)).astype(BF16)
            din = dot(w_s[sec], dpre_s[sec, :, at])
            hat = hat_s[sec, :, at]
            acc_s[sec, 0] += din * hat
            acc_s[sec, 1] += din
            f = din * wide(gain_s[sec, 0])
            up = up_s[sec, :, at] + (f - mean0(f) - hat * mean0(f * hat)) * inv_s[sec, 0:1, at]
            up_s[sec - 1 if sec > 0 else 2, :, at] = up
            return carry

        lax.fori_loop(0, 4, block, 0)

    def back_to_cells(sec):
        def block(b, carry):
            lanes_to_cells(up_s[sec - 1 if sec > 0 else 2, :, lanes(b)], pgb.at[sec], b)
            return carry

        lax.fori_loop(0, 4, block, 0)

    def early_grads(sec):
        g = dot(nrm_s[sec], dpre_s[sec, 512:640, :], 1, 1)
        gs[sec, 32:40] = g.reshape(8, 16, 128).astype(BF16)
        g = dot(mn_s[sec], dout_s[sec], 1, 1)
        gs[sec, 40:48] = g.reshape(8, 16, 128).astype(BF16)
        scatter_grads(sec, True)

    def late_grads(sec):
        for o in range(4):
            g = dot(nrm_s[sec], dpre_s[sec, 128 * o:128 * o + 128, :], 1, 1)
            gs[sec, 8 * o:8 * o + 8] = g.reshape(8, 16, 128).astype(BF16)
        rows = []
        for v in range(4):
            total = (acc_s[sec, v, :, 0:128] + acc_s[sec, v, :, 128:256]).T
            rows.append(jnp.sum(total, axis=0, keepdims=True))
        rows = jnp.concatenate(rows + [jnp.zeros((4, 128), F32)], axis=0)
        high = rows.astype(BF16).astype(F32)
        gs[sec, 48] = jnp.concatenate([high, rows - high], axis=0).astype(BF16)
        scatter_grads(sec, False)

    def scatter_grads(sec, early):
        def give(to_r, to_c):
            d = to_r * COLS + to_c
            mine = jnp.logical_and(m == sec, d == me)

            @pl.when(jnp.logical_not(mine))
            def _():
                pltpu.make_async_remote_copy(
                    gs.at[sec, d], recv_b.at[m * PEERS + me], ssem.at[RS, sec], rsem.at[RS, 0],
                    device_id=(sec, to_r, to_c), device_id_type=MESH,
                ).start()

            @pl.when(mine)
            def _():
                recv_b[m * PEERS + me] = gs[sec, d]

        def send(k, carry):
            to_c = column(k)
            if early:
                give(2, to_c)
            else:
                give(0, to_c)
                give(1, to_c)
            return carry

        lax.fori_loop(0, COLS, send, 0)
        if not early:
            give(3, 0)

    def gather_grads():
        @pl.when(me < OWNERS)
        def _():
            part = recv_b.at[pl.ds(0, 2 * PEERS - 1)]
            pltpu.make_async_copy(part, part, rsem.at[RS, 0]).wait()
            total = jnp.sum(recv_b[...].astype(F32), axis=0)
            vectors = total[0:8] + total[8:16]
            high = vectors.astype(BF16).astype(F32)
            split = jnp.concatenate([high, vectors - high], axis=0)
            recv_o[me] = jnp.where(me == OWNERS - 1, split, total).astype(BF16)

            def give(to_r, to_c):
                pltpu.make_async_remote_copy(
                    recv_o.at[me], recv_o.at[me], dsem.at[0], dsem.at[1],
                    device_id=(m, to_r, to_c), device_id_type=MESH,
                ).start()

            each_peer(give, False)

    prepare(m)
    loads[1].wait()
    front(m, act_s.at[other], False, other)
    loads[0].wait()
    pl.semaphore_wait(barrier, 2 * PEERS - 1)

    @pl.when(m == 1)
    def _():
        exchange_lr(to_own=False)

    swaps = [
        pltpu.make_async_remote_copy(
            src, dst, psend.at[n], precv.at[n], device_id=partner, device_id_type=MESH
        )
        for n, (src, dst) in enumerate(
            [(act_s.at[other], xs.at[m]), (w_s.at[m], w_s.at[m]), (wo_s.at[m], wo_s.at[m]), (vec_s.at[m], vec_s.at[m])]
        )
    ]
    for swap in swaps:
        swap.start()

    front(m, act_s.at[m], True, m)

    @pl.when(m == 1)
    def _():
        exchange_lr(to_other=False)

    def turn(b, carry):
        up_s[1, :, lanes(b)] = cells_to_lanes(cot_s, b)
        return carry

    loads[2].wait()
    lax.fori_loop(0, 4, turn, 0)
    for swap in swaps:
        swap.wait_recv()
    prepare(other)
    front(other, xs.at[other], True, None)
    out_before(1)

    mix(1)

    @pl.when(m == 0)
    def _():
        exchange_lr()

    out_chain(1)
    mix(0)
    products_back(1)
    out_after(1)
    out_forward(0)
    in_part(1)
    out_backward(0)
    early_grads(1)
    late_grads(1)
    back_to_cells(1)
    kept = pltpu.make_async_copy(pgb.at[m], pg_ref.at[m], dsem.at[2])
    handed = pltpu.make_async_remote_copy(
        pgb.at[other], pg_ref.at[m], psend.at[PG_COPY], precv.at[PG_COPY], device_id=partner, device_id_type=MESH
    )

    @pl.when(m == 0)
    def _():
        handed.start()

    @pl.when(m == 1)
    def _():
        kept.start()

    products_back(0)
    early_grads(0)

    in_part(0)
    late_grads(0)
    back_to_cells(0)

    @pl.when(m == 1)
    def _():
        handed.start()

    @pl.when(m == 0)
    def _():
        kept.start()

    gather_grads()

    for src, phase in ((send_m, MIX), (send_d, DMIX), (send_g, DLR)):
        for sec in range(2):
            sent(src, phase, sec)
    sent(send_lr, LR, m)
    part = send_lr.at[other]
    pltpu.make_async_copy(part, part, ssem.at[LR, other]).wait()
    for sec in range(2):
        own_rows = jnp.logical_and(m == sec, me < OWNERS)
        for count, which in ((OWNERS - 1, own_rows), (OWNERS, jnp.logical_not(own_rows))):

            @pl.when(which)
            def _(count=count, sec=sec):
                part = gs.at[sec, pl.ds(0, count)]
                pltpu.make_async_copy(part, part, ssem.at[RS, sec]).wait()

    for swap in swaps:
        swap.wait_send()
    handed.wait()
    kept.wait()

    @pl.when(me >= OWNERS)
    def _():
        part = recv_o.at[pl.ds(0, OWNERS)]
        pltpu.make_async_copy(part, part, dsem.at[1]).wait()

    @pl.when(me < OWNERS)
    def _():
        part = recv_o.at[pl.ds(0, OWNERS - 1)]
        pltpu.make_async_copy(part, part, dsem.at[1]).wait()
        part = recv_o.at[pl.ds(0, PEERS - 1)]
        pltpu.make_async_copy(part, part, dsem.at[0]).wait()


def write_out(pg_in, o_in, pg_ref, glng_ref, glnb_ref, gproj_ref, ggate_ref, gog_ref, gob_ref, gow_ref, held, o_ref, sem_in, sem_out, sem_o):
    rows = pltpu.make_async_copy(o_in.at[pl.ds(0, OWNERS)], o_ref, sem_o.at[0])
    parts = [pl.ds(n * 256, 256) for n in range(8)]
    come = [pltpu.make_async_copy(pg_in.at[p], held.at[p], sem_in.at[n]) for n, p in enumerate(parts)]
    go = [pltpu.make_async_copy(held.at[p], pg_ref.at[p], sem_out.at[n]) for n, p in enumerate(parts)]
    for copy in come:
        copy.start()
    rows.start()
    for copy_in, copy_out in zip(come, go):
        copy_in.wait()
        copy_out.start()
    rows.wait()
    for o in range(4):
        gproj_ref[:, 128 * o:128 * o + 128] = o_ref[8 * o:8 * o + 8].astype(F32).reshape(128, 128)
    ggate_ref[...] = o_ref[32:40].astype(F32).reshape(128, 128)
    gow_ref[...] = o_ref[40:48].astype(F32).reshape(128, 128)
    vectors = o_ref[48].astype(F32)
    for v, ref in enumerate((glng_ref, glnb_ref, gog_ref, gob_ref)):
        ref[...] = vectors[v:v + 1] + vectors[8 + v:9 + v]
    for copy in go:
        copy.wait()


def on_device(act, cot, mask, lng, lnb, proj, gatew, og, ob, outw):
    vmem = pl.BlockSpec(memory_space=pltpu.VMEM)
    anywhere = pl.BlockSpec(memory_space=pl.ANY)

    def v(shape, dtype=F32):
        return pltpu.VMEM(shape, dtype)

    sds = jax.ShapeDtypeStruct
    pg, rows = pl.pallas_call(
        kernel,
        out_shape=(sds((2, N, 128), F32), sds((PEERS, 16, 128), BF16)),
        in_specs=[anywhere] * 10,
        out_specs=(anywhere, vmem),
        scratch_shapes=[
            v((2, N, 128), BF16), v((N, 128)), v((2, 256), jnp.int32), pltpu.SMEM((2, 256), jnp.int32),
            v((2, N, 128), BF16), v((2, 128, 640), BF16), v((2, 128, 128), BF16), v((2, 8, 128)), v((N, 128)),
            v((2, 640, 128), BF16), v((2, 128, 128), BF16), v((2, 4, 128, 128)), v((2, 8, N)),
            v((2, 128, N)), v((2, 8, N)), v((2, 128, N), BF16),
            v((2, 128, N)), v((2, 128, N)), v((2, 128, N)), v((2, 128, N)), v((2, 128, N)),
            v((2, 128, N)), v((2, 8, N)), v((2, 128, N), BF16), v((2, 128, N)), v((3, 128, N)),
            v((2, 128, N), BF16), v((2, 640, N), BF16), v((2, 4, 128, WIDE)),
            v((128, N)), v((N, 128)), v((N, 128)), v((4, 256, 256), BF16), v((4, 256, 256), BF16), v((2, 256, 256), BF16),
            v((2, PEERS, 32, 128), BF16), v((2, PEERS, 32, 128), BF16),
            v((2, PEERS, 16, 128), BF16), v((2, PEERS, 16, 128), BF16),
            v((2, PEERS, 16, 128), BF16), v((2, PEERS, 16, 128), BF16),
            v((2, PEERS, 32, 128), BF16), v((2, PEERS, 32, 128), BF16),
            v((2, N, 128)), v((2, OWNERS, 16, 128), BF16), v((2 * PEERS, 16, 128), BF16),
            pltpu.SemaphoreType.DMA((12,)), pltpu.SemaphoreType.DMA((5,)), pltpu.SemaphoreType.DMA((5,)),
            pltpu.SemaphoreType.DMA((5, 2)), pltpu.SemaphoreType.DMA((5, 2)),
            pltpu.SemaphoreType.DMA((3,)),
        ],
        compiler_params=pltpu.CompilerParams(
            collective_id=1, has_side_effects=True, vmem_limit_bytes=56 * 2**20
        ),
    )(
        act.reshape(2, N, 128), cot.reshape(2, N, 128), mask, lng, lnb, proj[0], gatew[0], og, ob, outw[0]
    )
    pg, glng, glnb, gproj, ggate, gog, gob, gow = pl.pallas_call(
        write_out,
        out_shape=(
            sds((2 * N, 128), F32), sds((1, 128), F32), sds((1, 128), F32), sds((128, 512), F32),
            sds((128, 128), F32), sds((1, 128), F32), sds((1, 128), F32), sds((128, 128), F32),
        ),
        in_specs=[anywhere, anywhere],
        out_specs=(anywhere,) + (vmem,) * 7,
        scratch_shapes=[
            v((2 * N, 128)), v((OWNERS, 16, 128), BF16),
            pltpu.SemaphoreType.DMA((8,)), pltpu.SemaphoreType.DMA((8,)), pltpu.SemaphoreType.DMA((1,)),
        ],
    )(pg.reshape(2 * N, 128), rows)
    return (
        pg.reshape(1, 2, 64, 16, 128), glng, glnb, gproj[None], ggate[None], gog, gob, gow[None],
    )


def solution(mesh):
    vector, matrix = P("section", None), P("section", None, None)
    grid = P("section", None, "row", "col", None)
    return jax.shard_map(
        on_device,
        mesh=mesh,
        in_specs=(grid, P(None, "row", "col", None), P(), vector, vector, matrix, matrix, vector, vector, matrix),
        out_specs=(grid, vector, vector, matrix, matrix, vector, vector, matrix),
        check_vma=False,
    )
```

```python
import jax
import jax.numpy as jnp
from jax import lax
from jax.experimental import pallas as pl
from jax.experimental.pallas import tpu as pltpu
from jax.sharding import PartitionSpec as P

EPSILON = 1e-05
MESH = pl.DeviceIdType.MESH
F32 = jnp.float32
BF16 = jnp.bfloat16
ROWS = 4
COLS = 16
PEERS = ROWS * COLS
N = 1024
WIDE = 256

X_COPY, W_COPY, O_COPY, V_COPY, PG_COPY = range(5)
LR, MIX, DMIX, DLR, RS = range(5)
OWNERS = 49


def sigmoid(v):
    return 0.5 * jnp.tanh(0.5 * v) + 0.5


def mean0(v):
    return jnp.mean(v, axis=0, keepdims=True)


def dot(a, b, ca=1, cb=0):
    return lax.dot_general(a, b, (((ca,), (cb,)), ((), ())), preferred_element_type=F32)


def kernel(
    act_ref, cot_ref, mask_ref, lng_ref, lnb_ref, proj_ref, gatew_ref, og_ref, ob_ref, outw_ref,
    pg_ref, recv_o,
    act_s, cot_s, mask_v, mask_sm, xs, w_s, wo_s, vec_s, xf, wt_s, wot_s, gain_s, mask_s,
    hat_s, inv_s, nrm_s, la_s, ga_s, lb_s, gb_s, go_s,
    mhat_s, minv_s, mn_s, oc_s, up_s, dout_s, dpre_s, acc_s,
    dn_s, scr_a, scr_b, lt_s, rt_s, dt_s,
    send_lr, recv_lr, send_m, recv_m, send_d, recv_d, send_g, recv_g,
    pgb, gs, recv_b,
    isem, psend, precv, ssem, rsem, dsem,
):
    m, r, c = lax.axis_index("section"), lax.axis_index("row"), lax.axis_index("col")
    me = r * COLS + c
    other = 1 - m
    partner = (other, r, c)

    z, y = c // 4, lax.rem(c, 4)

    def step4(v):
        return jnp.where(v == 0, 2, jnp.where(v == 3, 0, 2 * v - 1))

    def column(k):
        return lax.rem(z + step4(k // 4), 4) * 4 + lax.rem(y + step4(lax.rem(k, 4)), 4)

    def each_peer(visit, with_own_place):
        def four(k, carry):
            to_c = column(k)
            for step in (2, 1, 3):
                visit(lax.rem(r + step, 4), to_c)
            if with_own_place:
                visit(r, to_c)
            else:
                pl.when(k < COLS - 1)(lambda: visit(r, to_c))
            return carry

        lax.fori_loop(0, COLS, four, 0)

    loads = [
        pltpu.make_async_copy(src, dst, isem.at[n])
        for n, (src, dst) in enumerate(
            [
                (act_ref.at[m], act_s.at[m]), (act_ref.at[other], act_s.at[other]), (cot_ref.at[m], cot_s),
                (proj_ref, w_s.at[m, :, pl.ds(0, 512)]), (gatew_ref, w_s.at[m, :, pl.ds(512, 128)]), (outw_ref, wo_s.at[m]),
                (lng_ref, vec_s.at[m, pl.ds(0, 1)]), (lnb_ref, vec_s.at[m, pl.ds(1, 1)]),
                (og_ref, vec_s.at[m, pl.ds(2, 1)]), (ob_ref, vec_s.at[m, pl.ds(3, 1)]),
                (mask_ref, mask_v), (mask_ref, mask_sm),
            ]
        )
    ]
    barrier = pltpu.get_barrier_semaphore()

    def greet(core):
        def visit(to_r, to_c):
            pl.semaphore_signal(barrier, inc=1, device_id=(core, to_r, to_c), device_id_type=MESH)

        return visit

    @pl.when(m == 0)
    def _():
        each_peer(greet(other), True)
        each_peer(greet(m), False)

    @pl.when(m == 1)
    def _():
        each_peer(greet(m), False)
        each_peer(greet(other), True)

    for load in loads:
        load.start()

    for load in loads[3:]:
        load.wait()
    vec_s[m, 4:8] = jnp.zeros((4, 128), F32)

    low = lax.broadcasted_iota(jnp.int32, (128, 128), 1) < 64
    low1 = lax.broadcasted_iota(jnp.int32, (8, 128), 1) < 64

    def exchange(src, dst, phase, sec):
        def send(to_r, to_c):
            pltpu.make_async_remote_copy(
                src.at[sec, to_r * COLS + to_c], dst.at[sec, me], ssem.at[phase, sec], rsem.at[phase, sec],
                device_id=(m, to_r, to_c), device_id_type=MESH,
            ).start()

        each_peer(send, False)
        dst[sec, me] = src[sec, me]

    def exchange_lr(to_other=True, to_own=True):
        def send(dest):
            def visit(to_r, to_c):
                pltpu.make_async_remote_copy(
                    send_lr.at[dest, to_r * COLS + to_c], recv_lr.at[m, me], ssem.at[LR, dest], rsem.at[LR, m],
                    device_id=(dest, to_r, to_c), device_id_type=MESH,
                ).start()

            return visit

        if to_other:
            each_peer(send(other), True)
        if to_own:
            each_peer(send(m), False)
            recv_lr[m, me] = send_lr[m, me]

    def arrived_lr(sec):
        @pl.when(m == sec)
        def _():
            arrived(recv_lr, LR, sec)

        @pl.when(m != sec)
        def _():
            part = recv_lr.at[sec]
            pltpu.make_async_copy(part, part, rsem.at[LR, sec]).wait()


    def arrived(dst, phase, sec):
        part = dst.at[sec, pl.ds(0, PEERS - 1)]
        pltpu.make_async_copy(part, part, rsem.at[phase, sec]).wait()

    def sent(src, phase, sec):
        part = src.at[sec, pl.ds(0, PEERS - 1)]
        pltpu.make_async_copy(part, part, ssem.at[phase, sec]).wait()

    def lanes(b):
        return pl.ds(pl.multiple_of(b * WIDE, WIDE), WIDE)

    def cells_to_lanes(src, b):
        out = []
        for u in range(2):
            t = 2 * b + u
            rows = jnp.concatenate([src[pl.ds(t, 64, stride=16), :], src[pl.ds(t + 8, 64, stride=16), :]], axis=0)
            out.append(rows.T)
        return jnp.concatenate(out, axis=1)

    def lanes_to_cells(value, dst, b):
        for u in range(2):
            t = 2 * b + u
            rows = value[:, 128 * u:128 * u + 128].T
            dst[pl.ds(t, 64, stride=16), :] = rows[:64]
            dst[pl.ds(t + 8, 64, stride=16), :] = rows[64:]

    def spread(value, dst, b):
        for u in range(2):
            dst[pl.ds(2 * b + u, 128, stride=8), :] = value[:, 128 * u:128 * u + 128]

    def gathered(src, b):
        return jnp.concatenate([src[pl.ds(2 * b + u, 128, stride=8), :] for u in range(2)], axis=1)

    def wide(g):
        return jnp.concatenate([g, g], axis=1)

    is_even = lax.rem(r, 2) == 0
    for n in range(2):
        whole = mask_v[n:n + 1, :].astype(F32)
        half = jnp.broadcast_to(jnp.where(r >= 2, whole[:, 128:], whole[:, :128]), (8, 128))
        turned = pltpu.roll(half, 64, 1)
        mask_i = jnp.where(low1, jnp.where(is_even, half, turned), jnp.where(is_even, turned, half))
        for t in range(8):
            first = mask_sm[n, c * 16 + t].astype(F32)
            second = mask_sm[n, c * 16 + 8 + t].astype(F32)
            mask_s[n, :, 128 * t:128 * t + 128] = mask_i * jnp.where(low1, first, second)

    def prepare(sec):
        wt_s[sec] = w_s[sec].astype(F32).T.astype(BF16)
        wot_s[sec] = wo_s[sec].astype(F32).T.astype(BF16)
        for v in range(4):
            gain_s[sec, v] = jnp.broadcast_to(vec_s[sec, v:v + 1, :], (128, 128)).T

    def front(sec, source, save, target):
        xf[...] = source[...].astype(F32)

        def block(b, carry):
            at = lanes(b)
            x = cells_to_lanes(xf, b)
            centred = x - mean0(x)
            inv = lax.rsqrt(mean0(centred * centred) + EPSILON)
            hat = centred * inv
            nrm = (hat * wide(gain_s[sec, 0]) + wide(gain_s[sec, 1])).astype(BF16)
            lin_a = dot(wt_s[sec, 0:128], nrm)
            gate_a = sigmoid(dot(wt_s[sec, 128:256], nrm))
            lin_b = dot(wt_s[sec, 256:384], nrm)
            gate_b = sigmoid(dot(wt_s[sec, 384:512], nrm))
            if target is not None:
                mask = mask_s[target, 0:1, at]
                spread(gate_a * lin_a * mask, scr_a, b)
                spread(gate_b * lin_b * mask, scr_b, b)
            if save:
                hat_s[sec, :, at] = hat
                inv_s[sec, :, at] = jnp.broadcast_to(inv, (8, WIDE))
                nrm_s[sec, :, at] = nrm
                la_s[sec, :, at] = lin_a
                ga_s[sec, :, at] = gate_a
                lb_s[sec, :, at] = lin_b
                gb_s[sec, :, at] = gate_b
                go_s[sec, :, at] = sigmoid(dot(wt_s[sec, 512:640], nrm))
            return carry

        lax.fori_loop(0, 4, block, 0)
        if target is not None:
            send_lr[target, :, 0:16, :] = scr_a[...].reshape(PEERS, 16, 128).astype(BF16)
            send_lr[target, :, 16:32, :] = scr_b[...].reshape(PEERS, 16, 128).astype(BF16)

    def assemble(src, sec, at, dst, first):
        for q in range(2):
            even = src[sec, 32 * q:32 * q + 16, at:at + 16, :].astype(F32)
            odd = src[sec, 32 * q + 16:32 * q + 32, at:at + 16, :].astype(F32)
            for ch in range(2):
                a = even[:, 8 * ch:8 * ch + 8, :].reshape(128, 128)
                b = odd[:, 8 * ch:8 * ch + 8, :].reshape(128, 128)
                k0 = jnp.where(low, a, pltpu.roll(b, 64, 1)).reshape(16, 1, 8, 128)
                k1 = jnp.where(low, pltpu.roll(a, 64, 1), b).reshape(16, 1, 8, 128)
                full = jnp.concatenate([k0, k1], axis=1).reshape(256, 128)
                dst[first + ch, :, 128 * q:128 * q + 128] = full.astype(BF16)

    def take_apart(pair, dst, sec, at):
        for q in range(2):
            evens, odds = [], []
            for y in pair:
                y4 = y[:, 128 * q:128 * q + 128].reshape(16, 2, 8, 128)
                y0 = y4[:, 0].reshape(128, 128)
                y1 = y4[:, 1].reshape(128, 128)
                evens.append(jnp.where(low, y0, pltpu.roll(y1, 64, 1)).reshape(16, 8, 128))
                odds.append(jnp.where(low, pltpu.roll(y0, 64, 1), y1).reshape(16, 8, 128))
            dst[sec, 32 * q:32 * q + 16, at:at + 16, :] = jnp.concatenate(evens, axis=1).astype(BF16)
            dst[sec, 32 * q + 16:32 * q + 32, at:at + 16, :] = jnp.concatenate(odds, axis=1).astype(BF16)

    def mix(sec):
        arrived_lr(sec)
        assemble(recv_lr, sec, 0, lt_s, 2 * sec)
        assemble(recv_lr, sec, 16, rt_s, 2 * sec)
        pair = [dot(rt_s[2 * sec + ch], lt_s[2 * sec + ch], 0, 0) for ch in range(2)]
        take_apart(pair, send_m, sec, 0)
        exchange(send_m, recv_m, MIX, sec)

    def out_forward(sec):
        arrived(recv_m, MIX, sec)
        scr_a[...] = recv_m[sec].astype(F32).reshape(N, 128)

        def block(b, carry):
            at = lanes(b)
            x = gathered(scr_a, b)
            centred = x - mean0(x)
            inv = lax.rsqrt(mean0(centred * centred) + EPSILON)
            hat = centred * inv
            mn = (hat * wide(gain_s[sec, 2]) + wide(gain_s[sec, 3])).astype(BF16)
            mhat_s[sec, :, at] = hat
            minv_s[sec, :, at] = jnp.broadcast_to(inv, (8, WIDE))
            mn_s[sec, :, at] = mn
            gate = go_s[sec, :, at]
            oc_s[sec, :, at] = dot(wot_s[sec], mn) * gate * (1.0 - gate)
            return carry

        lax.fori_loop(0, 4, block, 0)

    def out_backward(sec):
        def block(b, carry):
            at = lanes(b)
            dout = (up_s[sec, :, at] * go_s[sec, :, at]).astype(BF16)
            dout_s[sec, :, at] = dout
            dn = dot(wo_s[sec], dout)
            dn_s[:, at] = dn
            hat = mhat_s[sec, :, at]
            e = dn * wide(gain_s[sec, 2])
            spread((e - mean0(e) - hat * mean0(e * hat)) * minv_s[sec, 0:1, at], scr_b, b)
            return carry

        lax.fori_loop(0, 4, block, 0)
        send_d[sec] = scr_b[...].reshape(PEERS, 16, 128).astype(BF16)
        exchange(send_d, recv_d, DMIX, sec)
        acc_s[sec, 2] = jnp.zeros((128, WIDE), F32)
        acc_s[sec, 3] = jnp.zeros((128, WIDE), F32)

        def rest(b, carry):
            at = lanes(b)
            dpre_s[sec, 512:640, at] = (up_s[sec, :, at] * oc_s[sec, :, at]).astype(BF16)
            dn = dn_s[:, at]
            acc_s[sec, 2] += dn * mhat_s[sec, :, at]
            acc_s[sec, 3] += dn
            return carry

        lax.fori_loop(0, 4, rest, 0)

    def out_before(sec):
        def block(b, carry):
            at = lanes(b)
            dout = (up_s[sec, :, at] * go_s[sec, :, at]).astype(BF16)
            dout_s[sec, :, at] = dout
            dn_s[:, at] = dot(wo_s[sec], dout)
            return carry

        lax.fori_loop(0, 4, block, 0)

    def out_chain(sec):
        arrived(recv_m, MIX, sec)
        scr_a[...] = recv_m[sec].astype(F32).reshape(N, 128)

        def block(b, carry):
            at = lanes(b)
            x = gathered(scr_a, b)
            centred = x - mean0(x)
            inv = lax.rsqrt(mean0(centred * centred) + EPSILON)
            hat = centred * inv
            mhat_s[sec, :, at] = hat
            e = dn_s[:, at] * wide(gain_s[sec, 2])
            spread((e - mean0(e) - hat * mean0(e * hat)) * inv, scr_b, b)
            return carry

        lax.fori_loop(0, 4, block, 0)
        send_d[sec] = scr_b[...].reshape(PEERS, 16, 128).astype(BF16)
        exchange(send_d, recv_d, DMIX, sec)

    def out_after(sec):
        acc_s[sec, 2] = jnp.zeros((128, WIDE), F32)
        acc_s[sec, 3] = jnp.zeros((128, WIDE), F32)

        def block(b, carry):
            at = lanes(b)
            hat = mhat_s[sec, :, at]
            mn = (hat * wide(gain_s[sec, 2]) + wide(gain_s[sec, 3])).astype(BF16)
            mn_s[sec, :, at] = mn
            gate = go_s[sec, :, at]
            dgate = up_s[sec, :, at] * dot(wot_s[sec], mn) * gate * (1.0 - gate)
            dpre_s[sec, 512:640, at] = dgate.astype(BF16)
            dn = dn_s[:, at]
            acc_s[sec, 2] += dn * hat
            acc_s[sec, 3] += dn
            return carry

        lax.fori_loop(0, 4, block, 0)

    def products_back(sec):
        arrived(recv_d, DMIX, sec)
        assemble(recv_d, sec, 0, dt_s, 0)
        pair = [dot(rt_s[2 * sec + ch], dt_s[ch]) for ch in range(2)]
        take_apart(pair, send_g, sec, 0)
        pair = [dot(lt_s[2 * sec + ch], dt_s[ch], 1, 1) for ch in range(2)]
        take_apart(pair, send_g, sec, 16)
        exchange(send_g, recv_g, DLR, sec)

    def in_part(sec):
        acc_s[sec, 0] = jnp.zeros((128, WIDE), F32)
        acc_s[sec, 1] = jnp.zeros((128, WIDE), F32)
        arrived(recv_g, DLR, sec)
        scr_a[...] = recv_g[sec, :, 0:16, :].astype(F32).reshape(N, 128)
        scr_b[...] = recv_g[sec, :, 16:32, :].astype(F32).reshape(N, 128)

        def block(b, carry):
            at = lanes(b)
            mask = mask_s[m, 0:1, at]
            gate = ga_s[sec, :, at]
            dg = gathered(scr_a, b) * gate * mask
            dpre_s[sec, 0:128, at] = dg.astype(BF16)
            dpre_s[sec, 128:256, at] = (dg * la_s[sec, :, at] * (1.0 - gate)).astype(BF16)
            gate = gb_s[sec, :, at]
            dg = gathered(scr_b, b) * gate * mask
            dpre_s[sec, 256:384, at] = dg.astype(BF16)
            dpre_s[sec, 384:512, at] = (dg * lb_s[sec, :, at] * (1.0 - gate)).astype(BF16)
            din = dot(w_s[sec], dpre_s[sec, :, at])
            hat = hat_s[sec, :, at]
            acc_s[sec, 0] += din * hat
            acc_s[sec, 1] += din
            f = din * wide(gain_s[sec, 0])
            up = up_s[sec, :, at] + (f - mean0(f) - hat * mean0(f * hat)) * inv_s[sec, 0:1, at]
            up_s[sec - 1 if sec > 0 else 2, :, at] = up
            return carry

        lax.fori_loop(0, 4, block, 0)

    def back_to_cells(sec):
        def block(b, carry):
            lanes_to_cells(up_s[sec - 1 if sec > 0 else 2, :, lanes(b)], pgb.at[sec], b)
            return carry

        lax.fori_loop(0, 4, block, 0)

    def early_grads(sec):
        g = dot(nrm_s[sec], dpre_s[sec, 512:640, :], 1, 1)
        gs[sec, 32:40] = g.reshape(8, 16, 128).astype(BF16)
        g = dot(mn_s[sec], dout_s[sec], 1, 1)
        gs[sec, 40:48] = g.reshape(8, 16, 128).astype(BF16)
        scatter_grads(sec, True)

    def late_grads(sec):
        for o in range(4):
            g = dot(nrm_s[sec], dpre_s[sec, 128 * o:128 * o + 128, :], 1, 1)
            gs[sec, 8 * o:8 * o + 8] = g.reshape(8, 16, 128).astype(BF16)
        rows = []
        for v in range(4):
            total = (acc_s[sec, v, :, 0:128] + acc_s[sec, v, :, 128:256]).T
            rows.append(jnp.sum(total, axis=0, keepdims=True))
        rows = jnp.concatenate(rows + [jnp.zeros((4, 128), F32)], axis=0)
        high = rows.astype(BF16).astype(F32)
        gs[sec, 48] = jnp.concatenate([high, rows - high], axis=0).astype(BF16)
        scatter_grads(sec, False)

    def scatter_grads(sec, early):
        def give(to_r, to_c):
            d = to_r * COLS + to_c
            mine = jnp.logical_and(m == sec, d == me)

            @pl.when(jnp.logical_not(mine))
            def _():
                pltpu.make_async_remote_copy(
                    gs.at[sec, d], recv_b.at[m * PEERS + me], ssem.at[RS, sec], rsem.at[RS, 0],
                    device_id=(sec, to_r, to_c), device_id_type=MESH,
                ).start()

            @pl.when(mine)
            def _():
                recv_b[m * PEERS + me] = gs[sec, d]

        def send(k, carry):
            to_c = column(k)
            if early:
                give(2, to_c)
            else:
                give(0, to_c)
                give(1, to_c)
            return carry

        lax.fori_loop(0, COLS, send, 0)
        if not early:
            give(3, 0)

    def gather_grads():
        @pl.when(me < OWNERS)
        def _():
            part = recv_b.at[pl.ds(0, 2 * PEERS - 1)]
            pltpu.make_async_copy(part, part, rsem.at[RS, 0]).wait()
            total = jnp.sum(recv_b[...].astype(F32), axis=0)
            vectors = total[0:8] + total[8:16]
            high = vectors.astype(BF16).astype(F32)
            split = jnp.concatenate([high, vectors - high], axis=0)
            recv_o[me] = jnp.where(me == OWNERS - 1, split, total).astype(BF16)

            def give(to_r, to_c):
                pltpu.make_async_remote_copy(
                    recv_o.at[me], recv_o.at[me], dsem.at[0], dsem.at[1],
                    device_id=(m, to_r, to_c), device_id_type=MESH,
                ).start()

            each_peer(give, False)

    prepare(m)
    loads[1].wait()
    front(m, act_s.at[other], False, other)
    loads[0].wait()
    pl.semaphore_wait(barrier, 2 * PEERS - 1)

    @pl.when(m == 1)
    def _():
        exchange_lr(to_own=False)

    swaps = [
        pltpu.make_async_remote_copy(
            src, dst, psend.at[n], precv.at[n], device_id=partner, device_id_type=MESH
        )
        for n, (src, dst) in enumerate(
            [(act_s.at[other], xs.at[m]), (w_s.at[m], w_s.at[m]), (wo_s.at[m], wo_s.at[m]), (vec_s.at[m], vec_s.at[m])]
        )
    ]
    for swap in swaps:
        swap.start()

    front(m, act_s.at[m], True, m)

    @pl.when(m == 1)
    def _():
        exchange_lr(to_other=False)

    def turn(b, carry):
        up_s[1, :, lanes(b)] = cells_to_lanes(cot_s, b)
        return carry

    loads[2].wait()
    lax.fori_loop(0, 4, turn, 0)
    for swap in swaps:
        swap.wait_recv()
    prepare(other)
    front(other, xs.at[other], True, None)
    out_before(1)

    mix(1)

    @pl.when(m == 0)
    def _():
        exchange_lr(to_other=False)
        exchange_lr(to_own=False)

    out_chain(1)
    mix(0)
    products_back(1)
    out_after(1)
    out_forward(0)
    in_part(1)
    out_backward(0)
    early_grads(1)
    late_grads(1)
    early_grads(0)
    products_back(0)
    back_to_cells(1)
    kept = pltpu.make_async_copy(pgb.at[m], pg_ref.at[m], dsem.at[2])
    handed = pltpu.make_async_remote_copy(
        pgb.at[other], pg_ref.at[m], psend.at[PG_COPY], precv.at[PG_COPY], device_id=partner, device_id_type=MESH
    )

    @pl.when(m == 0)
    def _():
        handed.start()

    @pl.when(m == 1)
    def _():
        kept.start()


    in_part(0)
    late_grads(0)
    back_to_cells(0)

    @pl.when(m == 1)
    def _():
        handed.start()

    @pl.when(m == 0)
    def _():
        kept.start()

    gather_grads()

    for src, phase in ((send_m, MIX), (send_d, DMIX), (send_g, DLR)):
        for sec in range(2):
            sent(src, phase, sec)
    sent(send_lr, LR, m)
    part = send_lr.at[other]
    pltpu.make_async_copy(part, part, ssem.at[LR, other]).wait()
    for sec in range(2):
        own_rows = jnp.logical_and(m == sec, me < OWNERS)
        for count, which in ((OWNERS - 1, own_rows), (OWNERS, jnp.logical_not(own_rows))):

            @pl.when(which)
            def _(count=count, sec=sec):
                part = gs.at[sec, pl.ds(0, count)]
                pltpu.make_async_copy(part, part, ssem.at[RS, sec]).wait()

    for swap in swaps:
        swap.wait_send()
    handed.wait()
    kept.wait()

    @pl.when(me >= OWNERS)
    def _():
        part = recv_o.at[pl.ds(0, OWNERS)]
        pltpu.make_async_copy(part, part, dsem.at[1]).wait()

    @pl.when(me < OWNERS)
    def _():
        part = recv_o.at[pl.ds(0, OWNERS - 1)]
        pltpu.make_async_copy(part, part, dsem.at[1]).wait()
        part = recv_o.at[pl.ds(0, PEERS - 1)]
        pltpu.make_async_copy(part, part, dsem.at[0]).wait()


def write_out(pg_in, o_in, pg_ref, glng_ref, glnb_ref, gproj_ref, ggate_ref, gog_ref, gob_ref, gow_ref, held, o_ref, sem_in, sem_out, sem_o):
    rows = pltpu.make_async_copy(o_in.at[pl.ds(0, OWNERS)], o_ref, sem_o.at[0])
    parts = [pl.ds(n * 256, 256) for n in range(8)]
    come = [pltpu.make_async_copy(pg_in.at[p], held.at[p], sem_in.at[n]) for n, p in enumerate(parts)]
    go = [pltpu.make_async_copy(held.at[p], pg_ref.at[p], sem_out.at[n]) for n, p in enumerate(parts)]
    for copy in come:
        copy.start()
    rows.start()
    for copy_in, copy_out in zip(come, go):
        copy_in.wait()
        copy_out.start()
    rows.wait()
    for o in range(4):
        gproj_ref[:, 128 * o:128 * o + 128] = o_ref[8 * o:8 * o + 8].astype(F32).reshape(128, 128)
    ggate_ref[...] = o_ref[32:40].astype(F32).reshape(128, 128)
    gow_ref[...] = o_ref[40:48].astype(F32).reshape(128, 128)
    vectors = o_ref[48].astype(F32)
    for v, ref in enumerate((glng_ref, glnb_ref, gog_ref, gob_ref)):
        ref[...] = vectors[v:v + 1] + vectors[8 + v:9 + v]
    for copy in go:
        copy.wait()


def on_device(act, cot, mask, lng, lnb, proj, gatew, og, ob, outw):
    vmem = pl.BlockSpec(memory_space=pltpu.VMEM)
    anywhere = pl.BlockSpec(memory_space=pl.ANY)

    def v(shape, dtype=F32):
        return pltpu.VMEM(shape, dtype)

    sds = jax.ShapeDtypeStruct
    pg, rows = pl.pallas_call(
        kernel,
        out_shape=(sds((2, N, 128), F32), sds((PEERS, 16, 128), BF16)),
        in_specs=[anywhere] * 10,
        out_specs=(anywhere, vmem),
        scratch_shapes=[
            v((2, N, 128), BF16), v((N, 128)), v((2, 256), jnp.int32), pltpu.SMEM((2, 256), jnp.int32),
            v((2, N, 128), BF16), v((2, 128, 640), BF16), v((2, 128, 128), BF16), v((2, 8, 128)), v((N, 128)),
            v((2, 640, 128), BF16), v((2, 128, 128), BF16), v((2, 4, 128, 128)), v((2, 8, N)),
            v((2, 128, N)), v((2, 8, N)), v((2, 128, N), BF16),
            v((2, 128, N)), v((2, 128, N)), v((2, 128, N)), v((2, 128, N)), v((2, 128, N)),
            v((2, 128, N)), v((2, 8, N)), v((2, 128, N), BF16), v((2, 128, N)), v((3, 128, N)),
            v((2, 128, N), BF16), v((2, 640, N), BF16), v((2, 4, 128, WIDE)),
            v((128, N)), v((N, 128)), v((N, 128)), v((4, 256, 256), BF16), v((4, 256, 256), BF16), v((2, 256, 256), BF16),
            v((2, PEERS, 32, 128), BF16), v((2, PEERS, 32, 128), BF16),
            v((2, PEERS, 16, 128), BF16), v((2, PEERS, 16, 128), BF16),
            v((2, PEERS, 16, 128), BF16), v((2, PEERS, 16, 128), BF16),
            v((2, PEERS, 32, 128), BF16), v((2, PEERS, 32, 128), BF16),
            v((2, N, 128)), v((2, OWNERS, 16, 128), BF16), v((2 * PEERS, 16, 128), BF16),
            pltpu.SemaphoreType.DMA((12,)), pltpu.SemaphoreType.DMA((5,)), pltpu.SemaphoreType.DMA((5,)),
            pltpu.SemaphoreType.DMA((5, 2)), pltpu.SemaphoreType.DMA((5, 2)),
            pltpu.SemaphoreType.DMA((3,)),
        ],
        compiler_params=pltpu.CompilerParams(
            collective_id=1, has_side_effects=True, vmem_limit_bytes=56 * 2**20
        ),
    )(
        act.reshape(2, N, 128), cot.reshape(2, N, 128), mask, lng, lnb, proj[0], gatew[0], og, ob, outw[0]
    )
    pg, glng, glnb, gproj, ggate, gog, gob, gow = pl.pallas_call(
        write_out,
        out_shape=(
            sds((2 * N, 128), F32), sds((1, 128), F32), sds((1, 128), F32), sds((128, 512), F32),
            sds((128, 128), F32), sds((1, 128), F32), sds((1, 128), F32), sds((128, 128), F32),
        ),
        in_specs=[anywhere, anywhere],
        out_specs=(anywhere,) + (vmem,) * 7,
        scratch_shapes=[
            v((2 * N, 128)), v((OWNERS, 16, 128), BF16),
            pltpu.SemaphoreType.DMA((8,)), pltpu.SemaphoreType.DMA((8,)), pltpu.SemaphoreType.DMA((1,)),
        ],
    )(pg.reshape(2 * N, 128), rows)
    return (
        pg.reshape(1, 2, 64, 16, 128), glng, glnb, gproj[None], ggate[None], gog, gob, gow[None],
    )


def solution(mesh):
    vector, matrix = P("section", None), P("section", None, None)
    grid = P("section", None, "row", "col", None)
    return jax.shard_map(
        on_device,
        mesh=mesh,
        in_specs=(grid, P(None, "row", "col", None), P(), vector, vector, matrix, matrix, vector, vector, matrix),
        out_specs=(grid, vector, vector, matrix, matrix, vector, vector, matrix),
        check_vma=False,
    )
```
